32 devices in a mesh: dp: 32 (over z, y, x, core).
Axes of the slice: x: 2, y: 2, z: 4, core: 2. Of those that a mesh axis runs over, the one named last changes fastest.
Arguments:
- tokens: bfloat16 [24576, 256], P('dp'), may hold values from -6 to 6
- lengths: int32 [192], P('dp'), may hold values from 1 to 128, as said below
- w_qkv: bfloat16 [256, 768], P('dp'), may hold values from -0.375 to 0.375
- w_attn: bfloat16 [256, 256], P('dp'), may hold values from -0.75 to 0.75
- w_in: bfloat16 [256, 768], P('dp'), may hold values from -0.375 to 0.375
- w_mlp: bfloat16 [384, 256], P(None, 'dp'), may hold values from -0.3125 to 0.3125
- gain_attn: bfloat16 [256], P('dp'), may hold values from 0.5 to 1.5
- gain_mlp: bfloat16 [256], P('dp'), may hold values from 0.5 to 1.5
- cotangent: bfloat16 [24576, 256], P('dp'), may hold values from -6 to 6
Outputs:
- block_out: bfloat16 [24576, 256], P('dp')
- grad_tokens: float32 [24576, 256], P('dp')
- grad_qkv: float32 [256, 768], P('dp')
- grad_attn: float32 [256, 256], P('dp')
- grad_in: float32 [256, 768], P('dp')
- grad_mlp: float32 [384, 256], P(None, 'dp')
- grad_gain_attn: float32 [256], P('dp')
- grad_gain_mlp: float32 [256], P('dp')
The draws below stay inside these ranges and needn't reach their ends.
Inputs may be any that keep to these rules, and one draw needn't show every extreme that they name: `lengths`: entry i is the block of rows i * 128 to (i + 1) * 128 - 1; device d holds entries d * 3 * 2 onward, micro-batch m of it the 2 entries from m * 2.
All inputs are finite; a program needn't handle non-finite values.
Results may differ from the reference program's by a relative error of at most 0.011.
Values may be sent and summed in bfloat16 or wider, within the bound.
No kernel may reach another device: no remote copies, remote signals or barrier semaphores. Data moves between devices by JAX's collectives and lax.ppermute only.
A program may use at most 64 MiB of HBM per device.

```python
import jax
import jax.numpy as jnp
from jax import lax

D = 256
FF = 384
HEADS = 4
HEAD_DIM = 64
BLOCK = 128
MICRO = 3
BLOCKS = 2
CAP = 256
TOKENS = 24576
SEQS = 192
N_DP = 32


def draw_lengths(key, part):
    key = jax.random.fold_in(key, 11)
    key_low, key_bits, key_pick = jax.random.split(key, 3)
    per_device = MICRO * BLOCKS
    device_count = SEQS // per_device
    lowest = jax.random.randint(key_low, (device_count,), 1, BLOCK // 2 + 1)
    lowest = jnp.repeat(lowest, per_device, total_repeat_length=SEQS)
    random_bits = jax.random.randint(key_bits, (SEQS,), 0, 1 << 20)
    drawn = lowest + random_bits % (BLOCK + 1 - lowest)
    chosen = jax.random.randint(key_pick, (), 0, SEQS)
    drawn = jnp.where(jnp.arange(SEQS) == chosen, BLOCK, drawn)
    return drawn.astype(jnp.int32)


def shard_levels(own_key, extent, shards, least, top_value):
    gain = 1.0
    for axis_at, parts in shards:
        heights = jax.random.uniform(jax.random.fold_in(jax.random.fold_in(own_key, 6), axis_at), (parts,), jnp.float32, least / len(shards), top_value / len(shards))
        gain = gain * jnp.repeat(jnp.exp(heights), extent[axis_at] // parts).reshape((-1,) + (1,) * (len(extent) - 1 - axis_at))
    return gain


def gaussian(rng, dims, scale, bound, cuts=(), kind=jnp.bfloat16):
    entries = jax.random.normal(rng, dims, jnp.float32) * scale
    if len(cuts) > 0:
        entries = shard_levels(rng, dims, cuts, -0.22, 0.18) * entries
    return jnp.clip(entries, min=-bound, max=bound).astype(kind)


def setup_inputs(seed: int = 0) -> dict:
    arg_keys = jax.random.split(jax.random.key(seed), 10)
    tokens = gaussian(arg_keys[0], (TOKENS, D), 1.0, 6.0, ((0, 32),))
    lengths = draw_lengths(jax.random.fold_in(arg_keys[9], 71), 0)
    w_qkv = gaussian(arg_keys[2], (D, 3 * D), D ** -0.5, 0.375, ((0, 32),))
    w_attn = gaussian(arg_keys[3], (D, D), (D // 4) ** -0.5, 0.75, ((0, 32),))
    w_in = gaussian(arg_keys[4], (D, 2 * FF), D ** -0.5, 0.375, ((0, 32),))
    w_mlp = gaussian(arg_keys[5], (FF, D), FF ** -0.5, 0.3125, ((1, 32),))
    gain_attn = jnp.clip(1.0 + 0.1 * jax.random.normal(arg_keys[6], (D,), jnp.float32), 0.5, 1.5).astype(jnp.bfloat16)
    gain_mlp = jnp.clip(1.0 + 0.1 * jax.random.normal(arg_keys[7], (D,), jnp.float32), 0.5, 1.5).astype(jnp.bfloat16)
    cotangent = gaussian(arg_keys[8], (TOKENS, D), 1.0, 6.0, ((0, 32),))
    return dict(tokens=tokens, lengths=lengths, w_qkv=w_qkv, w_attn=w_attn, w_in=w_in, w_mlp=w_mlp, gain_attn=gain_attn, gain_mlp=gain_mlp, cotangent=cotangent)


@jax.custom_vjp
def low(v):
    return lax.optimization_barrier(v.astype(jnp.bfloat16)).astype(jnp.float32)

@jax.custom_vjp
def low_back(v):
    return v

def low_keep(v):
    return (low(v), None)

def low_pass(kept, grad):
    return (grad,)

def back_keep(v):
    return (v, None)

def back_low(kept, grad):
    return (low(grad),)
low.defvjp(low_keep, low_pass)
low_back.defvjp(back_keep, back_low)
rope_base = 160000.0
eps_norm = 1e-05
precise = lax.Precision.HIGHEST

def tables():
    half_dim = HEAD_DIM // 2
    frequency = rope_base ** (-(jnp.arange(half_dim, dtype=jnp.float32) * 2.0) / HEAD_DIM)
    angles = jnp.arange(BLOCK, dtype=jnp.float32)[:, None] * frequency[None, :]
    angles = jnp.concatenate([angles, angles], axis=1)
    return (jnp.cos(angles), jnp.sin(angles))

def rotate(values, cos_table, sine_table):
    half_dim = HEAD_DIM // 2
    turned = jnp.concatenate([-values[..., half_dim:], values[..., :half_dim]], axis=-1)
    return values * cos_table[None, :, None, :] + turned * sine_table[None, :, None, :]

def normalize(values, scale):
    centre = values - lax.optimization_barrier(jnp.mean(values, axis=-1, keepdims=True))
    spread = lax.optimization_barrier(jnp.mean(centre * centre, axis=-1, keepdims=True))
    return centre * lax.rsqrt(spread + eps_norm) * scale

def forward(token_rows, w_qkv, w_attn, w_in, w_mlp, gain_attn, gain_mlp, seq_lengths):
    block_count = seq_lengths.shape[0]
    score_scale = HEAD_DIM ** (-0.5)
    cos_table, sine_table = tables()
    normed = low(normalize(token_rows, gain_attn))
    merged = low_back(jnp.dot(normed, w_qkv, precision=precise))
    merged = merged.reshape(block_count, BLOCK, 3, HEADS, HEAD_DIM)
    queries = low(rotate(merged[:, :, 0], cos_table, sine_table))
    key_rows = low(rotate(merged[:, :, 1], cos_table, sine_table))
    value_rows = low(merged[:, :, 2])
    scores = low_back(jnp.einsum('bqhd,bkhd->bhqk', queries, key_rows, precision=precise) * score_scale)
    live_key = jnp.arange(BLOCK)[None, :] < seq_lengths[:, None]
    scores = jnp.where(live_key[:, None, None, :], scores, -1e+30)
    shares = low(jax.nn.softmax(scores, axis=-1))
    mixture = jnp.einsum('bhqk,bkhd->bqhd', shares, value_rows, precision=precise)
    mixture = low(low_back(mixture.reshape(block_count * BLOCK, D)))
    middle = token_rows + low_back(jnp.dot(mixture, w_attn, precision=precise))
    normed_two = low(normalize(middle, gain_mlp))
    merged_two = low_back(jnp.dot(normed_two, w_in, precision=precise))
    hidden = low(jax.nn.gelu(merged_two[:, :FF], approximate=False) * merged_two[:, FF:])
    branch = low_back(jnp.dot(hidden, w_mlp, precision=precise))
    live_row = live_key.reshape(-1, 1)
    return jnp.where(live_row, middle + branch, 0.0)

def reference(tokens, lengths, w_qkv, w_attn, w_in, w_mlp, gain_attn, gain_mlp, cotangent):
    per_device = MICRO * CAP
    rows_all = tokens.astype(jnp.float32).reshape(N_DP, per_device, D)
    cot_all = cotangent.astype(jnp.float32).reshape(N_DP, per_device, D)
    lengths_all = lengths.reshape(N_DP, MICRO * BLOCKS)
    params = (w_qkv.astype(jnp.float32), w_attn.astype(jnp.float32), w_in.astype(jnp.float32), w_mlp.astype(jnp.float32), gain_attn.astype(jnp.float32), gain_mlp.astype(jnp.float32))

    def per_step(totals, inputs):
        token_rows, cot_rows, seq_lengths = inputs

        def local_fn(rows_in, p_qkv, p_attn, p_in, p_mlp, p_gain_a, p_gain_m):
            return forward(rows_in, p_qkv, p_attn, p_in, p_mlp, p_gain_a, p_gain_m, seq_lengths)
        result, pullback = jax.vjp(local_fn, token_rows, *params)
        gradients = pullback(cot_rows)
        totals = tuple((total + added for total, added in zip(totals, gradients[1:])))
        return (totals, (result.astype(jnp.bfloat16), gradients[0]))
    zero_sums = tuple((jnp.zeros(param.shape, jnp.float32) for param in params))
    totals, (outputs, input_grads) = lax.scan(per_step, zero_sums, (rows_all, cot_all, lengths_all))
    return (outputs.reshape(TOKENS, D), input_grads.reshape(TOKENS, D), totals[0], totals[1], totals[2], totals[3], totals[4], totals[5])
```

```python
import functools

import jax
import jax.numpy as jnp
import numpy as np
from jax import lax
from jax.experimental import pallas as pl
from jax.experimental.pallas import tpu as pltpu
from jax.sharding import PartitionSpec as P

D = 256
FF = 384
HEADS = 4
HEAD_DIM = 64
BLOCK = 128
BLOCKS = 2
HALF = D // 2
WIDE = HEADS * BLOCK
QKV = 3 * D
LANES = 128
FIRST = QKV + D + LANES
SECOND = 2 * FF + FF
SUMS = QKV + D

rope_base = 160000.0
eps_norm = 1e-05
bf16 = jnp.bfloat16
f32 = jnp.float32


def tables():
    half_dim = HEAD_DIM // 2
    frequency = rope_base ** (-(np.arange(half_dim) * 2.0) / HEAD_DIM)
    angles = np.arange(BLOCK)[:, None] * frequency[None, :]
    angles = np.tile(angles, (BLOCKS, HEADS))
    return np.cos(angles).astype(np.float32), np.sin(angles).astype(np.float32)


def mm(left, right):
    return lax.dot_general(left, right, (((1,), (0,)), ((), ())), preferred_element_type=f32)


def mm_nt(left, right):
    return lax.dot_general(left, right, (((1,), (1,)), ((), ())), preferred_element_type=f32)


def mm_tn(left, right):
    return lax.dot_general(left, right, (((0,), (0,)), ((), ())), preferred_element_type=f32)


def spread_columns(forward):
    old = lax.broadcasted_iota(jnp.int32, (D, D), 0 if forward else 1)
    new = lax.broadcasted_iota(jnp.int32, (D, D), 1 if forward else 0)
    target = ((old // 32) % 2) * HALF + (old // HEAD_DIM) * 32 + old % 32
    return jnp.where(target == new, 1.0, 0.0).astype(bf16)


def to_column(row):
    size = row.shape[1]
    here = lax.broadcasted_iota(jnp.int32, (size, size), 0)
    there = lax.broadcasted_iota(jnp.int32, (size, size), 1)
    return jnp.sum(jnp.where(here == there, row, 0.0), axis=1, keepdims=True)


def to_row(column):
    size = column.shape[0]
    here = lax.broadcasted_iota(jnp.int32, (size, size), 0)
    there = lax.broadcasted_iota(jnp.int32, (size, size), 1)
    return jnp.sum(jnp.where(here == there, column, 0.0), axis=0, keepdims=True)


def pack_kernel(w_qkv, w_attn, w_in, w_mlp, gain_attn, gain_mlp, out):
    spread = spread_columns(True)
    out[:, :D] = mm(w_qkv[:, :D], spread).astype(bf16)
    out[:, D : 2 * D] = mm(w_qkv[:, D : 2 * D], spread).astype(bf16)
    out[:, 2 * D : QKV] = w_qkv[:, 2 * D :]
    out[:, QKV : QKV + D] = w_attn[...]
    lane = lax.broadcasted_iota(jnp.int32, (out.shape[0], LANES), 1)
    gains = jnp.where(lane == 0, to_column(gain_attn[...].astype(f32)), 0.0)
    gains = jnp.where(lane == 1, to_column(gain_mlp[...].astype(f32)), gains)
    out[:, QKV + D : FIRST] = gains.astype(bf16)
    out[:, FIRST : FIRST + 2 * FF] = w_in[...]
    out[:, FIRST + 2 * FF :] = w_mlp[...]


def end_kernel(kept, got, w_qkv, w_in, gain_attn, gain_mlp, g_qkv, g_attn, g_in, g_mlp, g_first, g_second):
    total = kept[...].astype(f32) + got[...].astype(f32)
    part = total[:, :QKV]
    g_qkv[...] = part
    g_first[...] = to_row(jnp.sum(part * w_qkv[...].astype(f32), axis=1, keepdims=True)) / gain_attn[...].astype(f32)
    g_attn[...] = total[:, QKV : QKV + D]
    part = total[:, QKV + D : QKV + D + 2 * FF]
    g_in[...] = part
    g_second[...] = to_row(jnp.sum(part * w_in[...].astype(f32), axis=1, keepdims=True)) / gain_mlp[...].astype(f32)
    g_mlp[...] = total[:, QKV + D + 2 * FF :]


def standardize(values):
    centre = values - jnp.mean(values, axis=-1, keepdims=True)
    inverse = lax.rsqrt(jnp.mean(centre * centre, axis=-1, keepdims=True) + eps_norm)
    return centre * inverse, inverse


def norm_back(d_hat, hat_rows, inverse):
    mean_one = jnp.mean(d_hat, axis=-1, keepdims=True)
    mean_two = jnp.mean(d_hat * hat_rows, axis=-1, keepdims=True)
    return inverse * (d_hat - mean_one - hat_rows * mean_two)


def stack_heads(rows, masks):
    return jnp.concatenate([rows * mask for mask in masks], axis=0)


def turn_heads(values):
    return jnp.concatenate(
        [values[:, h * BLOCK : (h + 1) * BLOCK].T for h in range(HEADS)], axis=1
    )


def slot_order(hops, rows, me, slot_axis):
    slots = lax.broadcasted_iota(jnp.int32, (D, D), slot_axis)
    place = slots // rows
    owner = jnp.full((D, D), me, jnp.int32)
    for bit, mask in enumerate(hops):
        owner = owner ^ (((place >> bit) & 1) * mask)
    found = owner * rows + slots % rows == lax.broadcasted_iota(jnp.int32, (D, D), 1 - slot_axis)
    return jnp.where(found, 1.0, 0.0).astype(bf16)


def head_masks():
    lane = lax.broadcasted_iota(jnp.int32, (1, D), 1)
    spread = [jnp.where((lane % HALF) // 32 == h, 1.0, 0.0).astype(bf16) for h in range(HEADS)]
    plain = [jnp.where(lane // HEAD_DIM == h, 1.0, 0.0).astype(bf16) for h in range(HEADS)]
    return spread, plain


def chunks(total):
    cap = BLOCKS * BLOCK
    return [(i, slice(i * cap, (i + 1) * cap)) for i in range(total // cap)]


def block_slices(start):
    return [slice(start + b * BLOCK, start + (b + 1) * BLOCK) for b in range(BLOCKS)]


def live_rows(lengths, index):
    row = lax.broadcasted_iota(jnp.int32, (BLOCK, 1), 0)
    live = [jnp.where(row < lengths[index * BLOCKS + b], 1.0, 0.0) for b in range(BLOCKS)]
    return jnp.concatenate(live, axis=0) > 0.5


def attend_kernel(
    hops, rows, me, lengths, tokens, packed, other, cos, sin, weights, w_attn, gains, normed, heads, shares, mixture
):
    order = slot_order(hops, rows, me[0], 1)
    ordered = mm(order[:, : D // 2], packed[...]) + mm(order[:, D // 2 :], other[...])
    weights[...] = ordered[:, :QKV].astype(bf16)
    w_attn[...] = ordered[:, QKV : QKV + D].astype(bf16)
    here = lax.broadcasted_iota(jnp.int32, (D, D), 0) == lax.broadcasted_iota(jnp.int32, (D, D), 1)
    for k in range(2):
        column = ordered[:, QKV + D + k : QKV + D + k + 1]
        gains[k : k + 1, :] = jnp.sum(jnp.where(here, column, 0.0), axis=0, keepdims=True)
    gain = gains[0:1, :]
    w_qkv = weights[...]
    c = cos[...]
    s = sin[...]
    spread_masks, plain_masks = head_masks()
    key_lane = lax.broadcasted_iota(jnp.int32, (1, BLOCK), 1)
    for index, part in chunks(tokens.shape[0]):
        low = (standardize(tokens[part].astype(f32))[0] * gain).astype(bf16)
        normed[part] = low
        qkv = mm(low, w_qkv)

        def rope(base):
            low, high = qkv[:, base : base + HALF], qkv[:, base + HALF : base + D]
            return jnp.concatenate([low * c - high * s, high * c + low * s], axis=1)

        heads[part, :D] = (rope(0) * HEAD_DIM ** (-0.5)).astype(bf16)
        heads[part, D : 2 * D] = rope(D).astype(bf16)
        heads[part, 2 * D :] = qkv[:, 2 * D :].astype(bf16)
        for b, block in enumerate(block_slices(part.start)):
            live = key_lane < lengths[index * BLOCKS + b]
            scores = mm_nt(heads[block, :D], stack_heads(heads[block, D : 2 * D], spread_masks))
            for h in range(HEADS):
                cut = slice(h * BLOCK, (h + 1) * BLOCK)
                one = jnp.where(live, scores[:, cut], -1e30)
                grown = jnp.exp(one - jnp.max(one, axis=1, keepdims=True))
                shares[block, cut] = grown * (1.0 / jnp.sum(grown, axis=1, keepdims=True))
            mixed = mm(shares[block].astype(bf16), stack_heads(heads[block, 2 * D :], plain_masks))
            mixture[block] = mixed.astype(bf16)


def feed_kernel(
    hops, rows, me, lengths, tokens, cot, packed, other, attn, gains, mixture,
    w_mlp, middle, hidden, d_middle, d_mixture, g_attn, sums, hat_two_low, out_low, d_att, d_merged,
):
    order = slot_order(hops, rows, me[0], 1)
    ordered = mm(order[:, : D // 2], packed[...]) + mm(order[:, D // 2 :], other[...])
    ordered = ordered.astype(bf16)
    w_attn = attn[...]
    w_in = ordered[:, : 2 * FF]
    w_mlp[...] = ordered[:, 2 * FF :]
    gain = gains[1:2, :]
    for index, part in chunks(tokens.shape[0]):
        mid = tokens[part].astype(f32) + mm(mixture[part], w_attn)
        middle[part] = mid
        hat_two, inv_two = standardize(mid)
        low = (hat_two * gain).astype(bf16)
        hat_two_low[part] = low
        merged = mm(low, w_in)
        inner = merged[:, :FF]
        gate = merged[:, FF:]
        cdf = 0.5 * (1.0 + lax.erf(inner * 0.7071067811865476))
        curved = inner * cdf
        slope = cdf + inner * jnp.exp(-0.5 * inner * inner) * 0.3989422804014327
        hidden[part] = (curved * gate).astype(bf16)
        out_grad = jnp.where(live_rows(lengths, index), cot[part].astype(f32), 0.0)
        out_low[part] = out_grad.astype(bf16)
        d_hidden = mm(out_low[part], w_mlp[...])
        d_merged[part, :FF] = (d_hidden * gate * slope).astype(bf16)
        d_merged[part, FF:] = (d_hidden * curved).astype(bf16)
        d_normed = mm_nt(d_merged[part], w_in)
        d_mid = out_grad + norm_back(d_normed * gain, hat_two, inv_two)
        d_middle[part] = d_mid
        d_att[part] = d_mid.astype(bf16)
        d_mixture[part] = mm_nt(d_att[part], w_attn).astype(bf16)
    order = slot_order(hops, rows, me[0], 0)
    total = mm_tn(hat_two_low[...], d_merged[...]).astype(bf16)
    sums[:, : 2 * FF] = mm(order, total).astype(bf16)
    total = mm_tn(out_low[...], hidden[...]).astype(bf16)
    sums[:, 2 * FF :] = mm(order, total).astype(bf16)
    g_attn[...] = mm_tn(mixture[...], d_att[...]).astype(bf16)


def attend_back_kernel(
    hops, rows, me, heads, shares, d_mixture, normed, g_attn, cos, sin, sums, d_qkv
):
    c = cos[...]
    s = sin[...]
    spread_masks, plain_masks = head_masks()

    def rope_back(grads):
        low, high = grads[:, :HALF], grads[:, HALF:]
        return jnp.concatenate([low * c + high * s, high * c - low * s], axis=1).astype(bf16)

    for index, part in chunks(heads.shape[0]):
        d_queries = []
        d_keys = []
        for block in block_slices(part.start):
            queries, key_rows, value_rows = heads[block, :D], heads[block, D : 2 * D], heads[block, 2 * D :]
            d_mixed = d_mixture[block]
            d_shares = mm_nt(d_mixed, stack_heads(value_rows, plain_masks))
            d_scores = []
            for h in range(HEADS):
                cut = slice(h * BLOCK, (h + 1) * BLOCK)
                one, d_one = shares[block, cut], d_shares[:, cut]
                d_one = one * (d_one - jnp.sum(one * d_one, axis=1, keepdims=True))
                d_scores.append(d_one.astype(bf16))
            d_scores = jnp.concatenate(d_scores, axis=1)
            d_queries.append(mm(d_scores, stack_heads(key_rows, spread_masks)))
            d_keys.append(mm(turn_heads(d_scores), stack_heads(queries, spread_masks)))
            d_values = mm(turn_heads(shares[block].astype(bf16)), stack_heads(d_mixed, plain_masks))
            d_qkv[block, 2 * D :] = d_values.astype(bf16)
        d_qkv[part, :D] = rope_back(jnp.concatenate(d_queries, axis=0) * HEAD_DIM ** (-0.5))
        d_qkv[part, D : 2 * D] = rope_back(jnp.concatenate(d_keys, axis=0))
    order = slot_order(hops, rows, me[0], 0)
    total = mm_tn(normed[...], d_qkv[...]).astype(bf16)
    placed = mm(order, total).astype(bf16)
    spread = spread_columns(False)
    sums[:, :D] = mm(placed[:, :D], spread).astype(bf16)
    sums[:, D : 2 * D] = mm(placed[:, D : 2 * D], spread).astype(bf16)
    sums[:, 2 * D : QKV] = placed[:, 2 * D :]
    sums[:, QKV:] = mm(order, g_attn[...]).astype(bf16)


def outputs_kernel(lengths, tokens, weights, gains, d_qkv, d_middle, middle, hidden, w_mlp, out, grad):
    gain = gains[0:1, :]
    for index, part in chunks(tokens.shape[0]):
        result = middle[part] + mm_nt(hidden[part], w_mlp[...])
        out[part] = jnp.where(live_rows(lengths, index), result, 0.0).astype(bf16)
        hat_one, inv_one = standardize(tokens[part].astype(f32))
        d_normed = mm_nt(d_qkv[part], weights[...])
        grad[part] = d_middle[part] + norm_back(d_normed * gain, hat_one, inv_one)


SMALL = pl.BlockSpec(memory_space=pltpu.SMEM)
NEAR = pl.BlockSpec(memory_space=pltpu.VMEM)


def call(kernel, in_specs, shapes, scratch=()):
    return pl.pallas_call(
        kernel,
        in_specs=in_specs,
        out_specs=[NEAR] * len(shapes),
        out_shape=[jax.ShapeDtypeStruct(shape, kind) for shape, kind in shapes],
        scratch_shapes=[pltpu.VMEM(shape, kind) for shape, kind in scratch],
        compiler_params=pltpu.CompilerParams(vmem_limit_bytes=32 * 1024 * 1024),
    )


def put(room, piece, slot, column=0):
    return lax.dynamic_update_slice(room, piece, (slot, 0, column))


def on_device(n, tokens, lengths, w_qkv, w_attn, w_in, w_mlp, gain_attn, gain_mlp, cotangent):
    rows = D // n
    count = tokens.shape[0]
    hops = []
    while 2 ** len(hops) < n:
        hops.append(n >> (len(hops) + 1))
    last = len(hops) - 1
    swapped = list(hops)
    joined = last
    if last > 1:
        swapped[last - 2], swapped[last - 1] = hops[last - 1], hops[last - 2]
        joined = last - 2
    hops, swapped = tuple(hops), tuple(swapped)
    gain_attn = gain_attn.reshape(1, rows)
    gain_mlp = gain_mlp.reshape(1, rows)

    def trade(values, mask):
        return lax.ppermute(values, "dp", [(i, i ^ mask) for i in range(n)])

    held = pl.pallas_call(
        pack_kernel, out_specs=NEAR, out_shape=jax.ShapeDtypeStruct((rows, FIRST + SECOND), bf16)
    )(w_qkv, w_attn, w_in, w_mlp.T, gain_attn, gain_mlp)
    room = put(jnp.zeros((2**joined, rows, FIRST + SECOND), bf16), held[None], 0)
    for k in range(joined):
        room = put(room, trade(room[: 2**k], hops[k]), 2**k)
    first = put(jnp.zeros((n // 2, rows, FIRST), bf16), room[:, :, :FIRST], 0)
    second = put(jnp.zeros((n // 2, rows, SECOND), bf16), room[:, :, FIRST:], 0)
    for k in range(joined, last):
        one, two = trade(first[: 2**k], hops[k]), trade(second[: 2**k], swapped[k])
        first, second = put(first, one, 2**k), put(second, two, 2**k)
    first_got, second_got = trade(first, 1), trade(second, 1)
    first = first.reshape(D // 2, FIRST), first_got.reshape(D // 2, FIRST)
    second = second.reshape(D // 2, SECOND), second_got.reshape(D // 2, SECOND)

    cos, sin = tables()
    cos, sin = jnp.asarray(cos), jnp.asarray(sin)
    me = lax.axis_index("dp").astype(jnp.int32).reshape(1)
    weights, attn, gains, normed, heads, shares, mixture = call(
        functools.partial(attend_kernel, hops, rows),
        [SMALL] * 2 + [NEAR] * 5,
        [((D, QKV), bf16), ((D, D), bf16), ((2, D), f32), ((count, D), bf16), ((count, QKV), bf16), ((count, WIDE), f32), ((count, D), bf16)],
    )(me, lengths, tokens, *first, cos, sin)
    w_mlp_all, middle, hidden, d_middle, d_mixture, g_attn, second_sums = call(
        functools.partial(feed_kernel, swapped, rows),
        [SMALL] * 2 + [NEAR] * 7,
        [((D, FF), bf16), ((count, D), f32), ((count, FF), bf16), ((count, D), f32), ((count, D), bf16), ((D, D), bf16), ((D, 3 * FF), bf16)],
        [((count, D), bf16), ((count, D), bf16), ((count, D), bf16), ((count, 2 * FF), bf16)],
    )(me, lengths, tokens, cotangent, *second, attn, gains, mixture)
    first_sums, d_qkv = call(
        functools.partial(attend_back_kernel, hops, rows),
        [SMALL] + [NEAR] * 7,
        [((D, SUMS), bf16), ((count, QKV), bf16)],
    )(me, heads, shares, d_mixture, normed, g_attn, cos, sin)
    out, grad = call(
        outputs_kernel, [SMALL] + [NEAR] * 8, [((count, D), bf16), ((count, D), f32)]
    )(lengths, tokens, weights, gains, d_qkv, d_middle, middle, hidden, w_mlp_all)

    def halve(kept, mask):
        half = kept.shape[0] // 2
        got = trade(kept[half:], mask)
        return (kept[:half].astype(f32) + got.astype(f32)).astype(bf16)

    first, second = first_sums.reshape(n, rows, SUMS), second_sums.reshape(n, rows, 3 * FF)
    for k in range(last, joined - 1, -1):
        first, second = halve(first, hops[k]), halve(second, swapped[k])
    kept = jnp.zeros((2**joined, rows, SUMS + 3 * FF), bf16)
    kept = put(put(kept, first, 0), second, 0, SUMS)
    for k in range(joined - 1, 0, -1):
        kept = halve(kept, hops[k])
    got = trade(kept[1], hops[0])
    g_qkv, g_attn, g_in, g_mlp, g_first, g_second = call(
        end_kernel,
        [NEAR] * 6,
        [((rows, QKV), f32), ((rows, D), f32), ((rows, 2 * FF), f32), ((rows, FF), f32), ((1, rows), f32), ((1, rows), f32)],
    )(kept[0], got, w_qkv, w_in, gain_attn, gain_mlp)
    return out, grad, g_qkv, g_attn, g_in, g_mlp.T, g_first.reshape(rows), g_second.reshape(rows)


def solution(mesh):
    rows = P("dp", None)
    return jax.shard_map(
        functools.partial(on_device, mesh.shape["dp"]),
        mesh=mesh,
        in_specs=(rows, P("dp"), rows, rows, rows, P(None, "dp"), P("dp"), P("dp"), rows),
        out_specs=(rows, rows, rows, rows, rows, P(None, "dp"), P("dp"), P("dp")),
        check_vma=False,
    )
```

```python
import functools

import jax
import jax.numpy as jnp
import numpy as np
from jax import lax
from jax.experimental import pallas as pl
from jax.experimental.pallas import tpu as pltpu
from jax.sharding import PartitionSpec as P

D = 256
FF = 384
HEADS = 4
HEAD_DIM = 64
BLOCK = 128
HALF = D // 2
WIDE = HEADS * BLOCK
QKV = 3 * D
LANES = 128
FIRST = QKV + D + LANES
SECOND = 2 * FF + FF
SUMS = QKV + D

rope_base = 160000.0
eps_norm = 1e-05
bf16 = jnp.bfloat16
f32 = jnp.float32


def tables():
    half_dim = HEAD_DIM // 2
    frequency = rope_base ** (-(np.arange(half_dim) * 2.0) / HEAD_DIM)
    angles = np.arange(BLOCK)[:, None] * frequency[None, :]
    angles = np.tile(angles, (1, HEADS))
    return np.cos(angles).astype(np.float32), np.sin(angles).astype(np.float32)


def mm(left, right):
    return lax.dot_general(left, right, (((1,), (0,)), ((), ())), preferred_element_type=f32)


def mm_nt(left, right):
    return lax.dot_general(left, right, (((1,), (1,)), ((), ())), preferred_element_type=f32)


def mm_tn(left, right):
    return lax.dot_general(left, right, (((0,), (0,)), ((), ())), preferred_element_type=f32)


def spread_columns(forward):
    old = lax.broadcasted_iota(jnp.int32, (D, D), 0 if forward else 1)
    new = lax.broadcasted_iota(jnp.int32, (D, D), 1 if forward else 0)
    target = ((old // 32) % 2) * HALF + (old // HEAD_DIM) * 32 + old % 32
    return jnp.where(target == new, 1.0, 0.0).astype(bf16)


def to_column(row):
    size = row.shape[1]
    here = lax.broadcasted_iota(jnp.int32, (size, size), 0)
    there = lax.broadcasted_iota(jnp.int32, (size, size), 1)
    return jnp.sum(jnp.where(here == there, row, 0.0), axis=1, keepdims=True)


def to_row(column):
    size = column.shape[0]
    here = lax.broadcasted_iota(jnp.int32, (size, size), 0)
    there = lax.broadcasted_iota(jnp.int32, (size, size), 1)
    return jnp.sum(jnp.where(here == there, column, 0.0), axis=0, keepdims=True)


def pack_kernel(w_qkv, w_attn, w_in, w_mlp, gain_attn, gain_mlp, out):
    spread = spread_columns(True)
    out[:, :D] = mm(w_qkv[:, :D], spread).astype(bf16)
    out[:, D : 2 * D] = mm(w_qkv[:, D : 2 * D], spread).astype(bf16)
    out[:, 2 * D : QKV] = w_qkv[:, 2 * D :]
    out[:, QKV : QKV + D] = w_attn[...]
    lane = lax.broadcasted_iota(jnp.int32, (out.shape[0], LANES), 1)
    gains = jnp.where(lane == 0, to_column(gain_attn[...].astype(f32)), 0.0)
    gains = jnp.where(lane == 1, to_column(gain_mlp[...].astype(f32)), gains)
    out[:, QKV + D : FIRST] = gains.astype(bf16)
    out[:, FIRST : FIRST + 2 * FF] = w_in[...]
    out[:, FIRST + 2 * FF :] = w_mlp[...]


def end_kernel(kept, got, w_qkv, w_in, gain_attn, gain_mlp, g_qkv, g_attn, g_in, g_mlp, g_first, g_second):
    total = kept[...].astype(f32) + got[...].astype(f32)
    part = total[:, :QKV]
    g_qkv[...] = part
    g_first[...] = to_row(jnp.sum(part * w_qkv[...].astype(f32), axis=1, keepdims=True)) / gain_attn[...].astype(f32)
    g_attn[...] = total[:, QKV : QKV + D]
    part = total[:, QKV + D : QKV + D + 2 * FF]
    g_in[...] = part
    g_second[...] = to_row(jnp.sum(part * w_in[...].astype(f32), axis=1, keepdims=True)) / gain_mlp[...].astype(f32)
    g_mlp[...] = total[:, QKV + D + 2 * FF :]


def standardize(values):
    centre = values - jnp.mean(values, axis=-1, keepdims=True)
    inverse = lax.rsqrt(jnp.mean(centre * centre, axis=-1, keepdims=True) + eps_norm)
    return centre * inverse, inverse


def norm_back(d_hat, hat_rows, inverse):
    mean_one = jnp.mean(d_hat, axis=-1, keepdims=True)
    mean_two = jnp.mean(d_hat * hat_rows, axis=-1, keepdims=True)
    return inverse * (d_hat - mean_one - hat_rows * mean_two)


def stack_heads(rows, masks):
    return jnp.concatenate([rows * mask for mask in masks], axis=0)


def turn_heads(values):
    return jnp.concatenate(
        [values[:, h * BLOCK : (h + 1) * BLOCK].T for h in range(HEADS)], axis=1
    )


def slot_order(hops, rows, me, slot_axis):
    slots = lax.broadcasted_iota(jnp.int32, (D, D), slot_axis)
    place = slots // rows
    owner = jnp.full((D, D), me, jnp.int32)
    for bit, mask in enumerate(hops):
        owner = owner ^ (((place >> bit) & 1) * mask)
    found = owner * rows + slots % rows == lax.broadcasted_iota(jnp.int32, (D, D), 1 - slot_axis)
    return jnp.where(found, 1.0, 0.0).astype(bf16)


def head_masks():
    lane = lax.broadcasted_iota(jnp.int32, (1, D), 1)
    spread = [jnp.where((lane % HALF) // 32 == h, 1.0, 0.0).astype(bf16) for h in range(HEADS)]
    plain = [jnp.where(lane // HEAD_DIM == h, 1.0, 0.0).astype(bf16) for h in range(HEADS)]
    return spread, plain


def live_rows(lengths, count):
    row = lax.broadcasted_iota(jnp.int32, (BLOCK, 1), 0)
    live = [jnp.where(row < lengths[b], 1.0, 0.0) for b in range(count // BLOCK)]
    return jnp.concatenate(live, axis=0) > 0.5


def attend_kernel(
    hops, rows, me, lengths, tokens, packed, other, cos, sin, weights, w_attn, gains, normed, heads, shares, mixture
):
    order = slot_order(hops, rows, me[0], 1)
    ordered = mm(order[:, : D // 2], packed[...]) + mm(order[:, D // 2 :], other[...])
    weights[...] = ordered[:, :QKV].astype(bf16)
    w_attn[...] = ordered[:, QKV : QKV + D].astype(bf16)
    here = lax.broadcasted_iota(jnp.int32, (D, D), 0) == lax.broadcasted_iota(jnp.int32, (D, D), 1)
    for k in range(2):
        column = ordered[:, QKV + D + k : QKV + D + k + 1]
        gains[k : k + 1, :] = jnp.sum(jnp.where(here, column, 0.0), axis=0, keepdims=True)
    gain = gains[0:1, :]
    w_qkv = weights[...]
    c, s = cos[...], sin[...]
    spread_masks, plain_masks = head_masks()
    key_lane = lax.broadcasted_iota(jnp.int32, (1, BLOCK), 1)
    count = tokens.shape[0] // BLOCK
    for part in [slice(b * BLOCK, (b + 1) * BLOCK) for b in range(count)]:
        normed[part] = (standardize(tokens[part].astype(f32))[0] * gain).astype(bf16)

    def rope(base):
        both = mm(normed[...], w_qkv[:, base : base + D])
        low, high = both[:, :HALF].reshape(count, BLOCK, HALF), both[:, HALF:].reshape(count, BLOCK, HALF)
        both = jnp.concatenate([low * c - high * s, high * c + low * s], axis=2)
        return both.reshape(count * BLOCK, D)

    heads[:, :D] = (rope(0) * HEAD_DIM ** (-0.5)).astype(bf16)
    heads[:, D : 2 * D] = rope(D).astype(bf16)
    heads[:, 2 * D :] = mm(normed[...], w_qkv[:, 2 * D :]).astype(bf16)
    parts = [slice(b * BLOCK, (b + 1) * BLOCK) for b in range(count)]
    for block in parts:
        shares[block] = mm_nt(heads[block, :D], stack_heads(heads[block, D : 2 * D], spread_masks))
    for b, block in enumerate(parts):
        live = key_lane < lengths[b]
        for h in range(HEADS):
            cut = slice(h * BLOCK, (h + 1) * BLOCK)
            one = jnp.where(live, shares[block, cut], -1e30)
            grown = jnp.exp(one - jnp.max(one, axis=1, keepdims=True))
            shares[block, cut] = grown * (1.0 / jnp.sum(grown, axis=1, keepdims=True))
    for block in parts:
        mixed = mm(shares[block].astype(bf16), stack_heads(heads[block, 2 * D :], plain_masks))
        mixture[block] = mixed.astype(bf16)


def feed_kernel(
    hops, rows, me, lengths, tokens, cot, packed, other, attn, gains, mixture,
    w_mlp, middle, hidden, d_middle, d_mixture, g_attn, sums, hat_two_low, out_low, d_att, d_merged,
):
    order = slot_order(hops, rows, me[0], 1)
    ordered = mm(order[:, : D // 2], packed[...]) + mm(order[:, D // 2 :], other[...])
    ordered = ordered.astype(bf16)
    w_attn = attn[...]
    w_in = ordered[:, : 2 * FF]
    w_mlp[...] = ordered[:, 2 * FF :]
    gain = gains[1:2, :]
    mid = tokens[...].astype(f32) + mm(mixture[...], w_attn)
    middle[...] = mid
    hat_two, inv_two = standardize(mid)
    hat_two_low[...] = (hat_two * gain).astype(bf16)
    merged = mm(hat_two_low[...], w_in)
    inner = merged[:, :FF]
    gate = merged[:, FF:]
    cdf = 0.5 * (1.0 + lax.erf(inner * 0.7071067811865476))
    curved = inner * cdf
    slope = cdf + inner * jnp.exp(-0.5 * inner * inner) * 0.3989422804014327
    hidden[...] = (curved * gate).astype(bf16)
    out_grad = jnp.where(live_rows(lengths, tokens.shape[0]), cot[...].astype(f32), 0.0)
    out_low[...] = out_grad.astype(bf16)
    d_hidden = mm(out_low[...], w_mlp[...])
    d_merged[:, :FF] = (d_hidden * gate * slope).astype(bf16)
    d_merged[:, FF:] = (d_hidden * curved).astype(bf16)
    d_normed = mm_nt(d_merged[...], w_in)
    d_mid = out_grad + norm_back(d_normed * gain, hat_two, inv_two)
    d_middle[...] = d_mid
    d_att[...] = d_mid.astype(bf16)
    d_mixture[...] = mm_nt(d_att[...], w_attn).astype(bf16)
    order = slot_order(hops, rows, me[0], 0)
    total = mm_tn(hat_two_low[...], d_merged[...]).astype(bf16)
    sums[:, : 2 * FF] = mm(order, total).astype(bf16)
    total = mm_tn(out_low[...], hidden[...]).astype(bf16)
    sums[:, 2 * FF :] = mm(order, total).astype(bf16)
    g_attn[...] = mm_tn(mixture[...], d_att[...]).astype(bf16)


def attend_back_kernel(
    hops, rows, me, heads, shares, d_mixture, normed, g_attn, cos, sin, sums, d_qkv
):
    c, s = cos[...], sin[...]
    spread_masks, plain_masks = head_masks()

    def rope_back(grads):
        low, high = grads[:, :HALF], grads[:, HALF:]
        return jnp.concatenate([low * c + high * s, high * c - low * s], axis=1).astype(bf16)

    parts = [slice(b * BLOCK, (b + 1) * BLOCK) for b in range(heads.shape[0] // BLOCK)]
    d_shares = [mm_nt(d_mixture[block], stack_heads(heads[block, 2 * D :], plain_masks)) for block in parts]
    d_values = [mm(turn_heads(shares[block].astype(bf16)), stack_heads(d_mixture[block], plain_masks)) for block in parts]
    for block, d_value in zip(parts, d_values):
        d_qkv[block, 2 * D :] = d_value.astype(bf16)
    d_scores = []
    for block, d_share in zip(parts, d_shares):
        pieces = []
        for h in range(HEADS):
            cut = slice(h * BLOCK, (h + 1) * BLOCK)
            one, d_one = shares[block, cut], d_share[:, cut]
            d_one = one * (d_one - jnp.sum(one * d_one, axis=1, keepdims=True))
            pieces.append(d_one.astype(bf16))
        d_scores.append(jnp.concatenate(pieces, axis=1))
    for block, d_score in zip(parts, d_scores):
        d_qkv[block, :D] = rope_back(mm(d_score, stack_heads(heads[block, D : 2 * D], spread_masks)) * HEAD_DIM ** (-0.5))
    for block, d_score in zip(parts, d_scores):
        d_qkv[block, D : 2 * D] = rope_back(mm(turn_heads(d_score), stack_heads(heads[block, :D], spread_masks)))
    order = slot_order(hops, rows, me[0], 0)
    total = mm_tn(normed[...], d_qkv[...]).astype(bf16)
    placed = mm(order, total).astype(bf16)
    spread = spread_columns(False)
    sums[:, :D] = mm(placed[:, :D], spread).astype(bf16)
    sums[:, D : 2 * D] = mm(placed[:, D : 2 * D], spread).astype(bf16)
    sums[:, 2 * D : QKV] = placed[:, 2 * D :]
    sums[:, QKV:] = mm(order, g_attn[...]).astype(bf16)


def outputs_kernel(lengths, tokens, weights, gains, d_qkv, d_middle, middle, hidden, w_mlp, out, grad):
    gain = gains[0:1, :]
    result = middle[...] + mm_nt(hidden[...], w_mlp[...])
    out[...] = jnp.where(live_rows(lengths, tokens.shape[0]), result, 0.0).astype(bf16)
    hat_one, inv_one = standardize(tokens[...].astype(f32))
    d_normed = mm_nt(d_qkv[...], weights[...])
    grad[...] = d_middle[...] + norm_back(d_normed * gain, hat_one, inv_one)


SMALL = pl.BlockSpec(memory_space=pltpu.SMEM)
NEAR = pl.BlockSpec(memory_space=pltpu.VMEM)


def call(kernel, in_specs, shapes, scratch=()):
    return pl.pallas_call(
        kernel,
        in_specs=in_specs,
        out_specs=[NEAR] * len(shapes),
        out_shape=[jax.ShapeDtypeStruct(shape, kind) for shape, kind in shapes],
        scratch_shapes=[pltpu.VMEM(shape, kind) for shape, kind in scratch],
        compiler_params=pltpu.CompilerParams(vmem_limit_bytes=32 * 1024 * 1024),
    )


def put(room, piece, slot, column=0):
    return lax.dynamic_update_slice(room, piece, (slot, 0, column))


def on_device(n, tokens, lengths, w_qkv, w_attn, w_in, w_mlp, gain_attn, gain_mlp, cotangent):
    rows = D // n
    count = tokens.shape[0]
    hops = []
    while 2 ** len(hops) < n:
        hops.append(n >> (len(hops) + 1))
    last = len(hops) - 1
    swapped = list(hops)
    joined = last
    if last > 1:
        swapped[last - 2], swapped[last - 1] = hops[last - 1], hops[last - 2]
        joined = last - 2
    hops, swapped = tuple(hops), tuple(swapped)
    gain_attn = gain_attn.reshape(1, rows)
    gain_mlp = gain_mlp.reshape(1, rows)

    def trade(values, mask):
        return lax.ppermute(values, "dp", [(i, i ^ mask) for i in range(n)])

    held = pl.pallas_call(
        pack_kernel, out_specs=NEAR, out_shape=jax.ShapeDtypeStruct((rows, FIRST + SECOND), bf16)
    )(w_qkv, w_attn, w_in, w_mlp.T, gain_attn, gain_mlp)
    room = put(jnp.zeros((2**joined, rows, FIRST + SECOND), bf16), held[None], 0)
    for k in range(joined):
        room = put(room, trade(room[: 2**k], hops[k]), 2**k)
    first = put(jnp.zeros((n // 2, rows, FIRST), bf16), room[:, :, :FIRST], 0)
    second = put(jnp.zeros((n // 2, rows, SECOND), bf16), room[:, :, FIRST:], 0)
    for k in range(joined, last):
        one, two = trade(first[: 2**k], hops[k]), trade(second[: 2**k], swapped[k])
        first, second = put(first, one, 2**k), put(second, two, 2**k)
    first_got, second_got = trade(first, 1), trade(second, 1)
    first = first.reshape(D // 2, FIRST), first_got.reshape(D // 2, FIRST)
    second = second.reshape(D // 2, SECOND), second_got.reshape(D // 2, SECOND)

    cos, sin = tables()
    cos, sin = jnp.asarray(cos), jnp.asarray(sin)
    me = lax.axis_index("dp").astype(jnp.int32).reshape(1)
    weights, attn, gains, normed, heads, shares, mixture = call(
        functools.partial(attend_kernel, hops, rows),
        [SMALL] * 2 + [NEAR] * 5,
        [((D, QKV), bf16), ((D, D), bf16), ((2, D), f32), ((count, D), bf16), ((count, QKV), bf16), ((count, WIDE), f32), ((count, D), bf16)],
    )(me, lengths, tokens, *first, cos, sin)
    w_mlp_all, middle, hidden, d_middle, d_mixture, g_attn, second_sums = call(
        functools.partial(feed_kernel, swapped, rows),
        [SMALL] * 2 + [NEAR] * 7,
        [((D, FF), bf16), ((count, D), f32), ((count, FF), bf16), ((count, D), f32), ((count, D), bf16), ((D, D), bf16), ((D, 3 * FF), bf16)],
        [((count, D), bf16), ((count, D), bf16), ((count, D), bf16), ((count, 2 * FF), bf16)],
    )(me, lengths, tokens, cotangent, *second, attn, gains, mixture)
    first_sums, d_qkv = call(
        functools.partial(attend_back_kernel, hops, rows),
        [SMALL] + [NEAR] * 7,
        [((D, SUMS), bf16), ((count, QKV), bf16)],
    )(me, heads, shares, d_mixture, normed, g_attn, cos, sin)
    out, grad = call(
        outputs_kernel, [SMALL] + [NEAR] * 8, [((count, D), bf16), ((count, D), f32)]
    )(lengths, tokens, weights, gains, d_qkv, d_middle, middle, hidden, w_mlp_all)

    def halve(kept, mask):
        half = kept.shape[0] // 2
        got = trade(kept[half:], mask)
        return (kept[:half].astype(f32) + got.astype(f32)).astype(bf16)

    first, second = first_sums.reshape(n, rows, SUMS), second_sums.reshape(n, rows, 3 * FF)
    for k in range(last, joined - 1, -1):
        first, second = halve(first, hops[k]), halve(second, swapped[k])
    kept = jnp.zeros((2**joined, rows, SUMS + 3 * FF), bf16)
    kept = put(put(kept, first, 0), second, 0, SUMS)
    for k in range(joined - 1, 0, -1):
        kept = halve(kept, hops[k])
    got = trade(kept[1], hops[0])
    g_qkv, g_attn, g_in, g_mlp, g_first, g_second = call(
        end_kernel,
        [NEAR] * 6,
        [((rows, QKV), f32), ((rows, D), f32), ((rows, 2 * FF), f32), ((rows, FF), f32), ((1, rows), f32), ((1, rows), f32)],
    )(kept[0], got, w_qkv, w_in, gain_attn, gain_mlp)
    return out, grad, g_qkv, g_attn, g_in, g_mlp.T, g_first.reshape(rows), g_second.reshape(rows)


def solution(mesh):
    rows = P("dp", None)
    return jax.shard_map(
        functools.partial(on_device, mesh.shape["dp"]),
        mesh=mesh,
        in_specs=(rows, P("dp"), rows, rows, rows, P(None, "dp"), P("dp"), P("dp"), rows),
        out_specs=(rows, rows, rows, rows, rows, P(None, "dp"), P("dp"), P("dp")),
        check_vma=False,
    )
```

```python
import functools

import jax
import jax.numpy as jnp
import numpy as np
from jax import lax
from jax.experimental import pallas as pl
from jax.experimental.pallas import tpu as pltpu
from jax.sharding import PartitionSpec as P

D = 256
FF = 384
HEADS = 4
HEAD_DIM = 64
BLOCK = 128
HALF = D // 2
WIDE = HEADS * BLOCK
QKV = 3 * D
LANES = 128
FIRST = QKV + D + LANES
SECOND = 2 * FF + FF
SUMS = QKV + D

rope_base = 160000.0
eps_norm = 1e-05
bf16 = jnp.bfloat16
f32 = jnp.float32


def tables():
    half_dim = HEAD_DIM // 2
    frequency = rope_base ** (-(np.arange(half_dim) * 2.0) / HEAD_DIM)
    angles = np.arange(BLOCK)[:, None] * frequency[None, :]
    angles = np.tile(angles, (1, HEADS))
    return np.cos(angles).astype(np.float32), np.sin(angles).astype(np.float32)


def mm(left, right):
    return lax.dot_general(left, right, (((1,), (0,)), ((), ())), preferred_element_type=f32)


def mm_nt(left, right):
    return lax.dot_general(left, right, (((1,), (1,)), ((), ())), preferred_element_type=f32)


def mm_tn(left, right):
    return lax.dot_general(left, right, (((0,), (0,)), ((), ())), preferred_element_type=f32)


def spread_columns(forward):
    old = lax.broadcasted_iota(jnp.int32, (D, D), 0 if forward else 1)
    new = lax.broadcasted_iota(jnp.int32, (D, D), 1 if forward else 0)
    target = ((old // 32) % 2) * HALF + (old // HEAD_DIM) * 32 + old % 32
    return jnp.where(target == new, 1.0, 0.0).astype(bf16)


def to_column(row):
    size = row.shape[1]
    here = lax.broadcasted_iota(jnp.int32, (size, size), 0)
    there = lax.broadcasted_iota(jnp.int32, (size, size), 1)
    return jnp.sum(jnp.where(here == there, row, 0.0), axis=1, keepdims=True)


def to_row(column):
    size = column.shape[0]
    here = lax.broadcasted_iota(jnp.int32, (size, size), 0)
    there = lax.broadcasted_iota(jnp.int32, (size, size), 1)
    return jnp.sum(jnp.where(here == there, column, 0.0), axis=0, keepdims=True)


def pack_kernel(w_qkv, w_attn, w_in, w_mlp, gain_attn, gain_mlp, out):
    spread = spread_columns(True)
    out[:, :D] = mm(w_qkv[:, :D], spread).astype(bf16)
    out[:, D : 2 * D] = mm(w_qkv[:, D : 2 * D], spread).astype(bf16)
    out[:, 2 * D : QKV] = w_qkv[:, 2 * D :]
    out[:, QKV : QKV + D] = w_attn[...]
    lane = lax.broadcasted_iota(jnp.int32, (out.shape[0], LANES), 1)
    gains = jnp.where(lane == 0, to_column(gain_attn[...].astype(f32)), 0.0)
    gains = jnp.where(lane == 1, to_column(gain_mlp[...].astype(f32)), gains)
    out[:, QKV + D : FIRST] = gains.astype(bf16)
    out[:, FIRST : FIRST + 2 * FF] = w_in[...]
    out[:, FIRST + 2 * FF :] = w_mlp[...]


def end_kernel(kept, got, w_qkv, w_in, gain_attn, gain_mlp, g_qkv, g_attn, g_in, g_mlp, g_first, g_second):
    total = kept[...].astype(f32) + got[...].astype(f32)
    part = total[:, :QKV]
    g_qkv[...] = part
    g_first[...] = to_row(jnp.sum(part * w_qkv[...].astype(f32), axis=1, keepdims=True)) / gain_attn[...].astype(f32)
    g_attn[...] = total[:, QKV : QKV + D]
    part = total[:, QKV + D : QKV + D + 2 * FF]
    g_in[...] = part
    g_second[...] = to_row(jnp.sum(part * w_in[...].astype(f32), axis=1, keepdims=True)) / gain_mlp[...].astype(f32)
    g_mlp[...] = total[:, QKV + D + 2 * FF :]


def standardize(values):
    centre = values - jnp.mean(values, axis=-1, keepdims=True)
    inverse = lax.rsqrt(jnp.mean(centre * centre, axis=-1, keepdims=True) + eps_norm)
    return centre * inverse, inverse


def norm_back(d_hat, hat_rows, inverse):
    mean_one = jnp.mean(d_hat, axis=-1, keepdims=True)
    mean_two = jnp.mean(d_hat * hat_rows, axis=-1, keepdims=True)
    return inverse * (d_hat - mean_one - hat_rows * mean_two)


def stack_heads(rows, masks):
    return jnp.concatenate([rows * mask for mask in masks], axis=0)


def turn_heads(values):
    return jnp.concatenate(
        [values[:, h * BLOCK : (h + 1) * BLOCK].T for h in range(HEADS)], axis=1
    )


def slot_order(hops, rows, me, slot_axis):
    slots = lax.broadcasted_iota(jnp.int32, (D, D), slot_axis)
    place = slots // rows
    owner = jnp.full((D, D), me, jnp.int32)
    for bit, mask in enumerate(hops):
        owner = owner ^ (((place >> bit) & 1) * mask)
    found = owner * rows + slots % rows == lax.broadcasted_iota(jnp.int32, (D, D), 1 - slot_axis)
    return jnp.where(found, 1.0, 0.0).astype(bf16)


def head_masks():
    lane = lax.broadcasted_iota(jnp.int32, (1, D), 1)
    spread = [jnp.where((lane % HALF) // 32 == h, 1.0, 0.0).astype(bf16) for h in range(HEADS)]
    plain = [jnp.where(lane // HEAD_DIM == h, 1.0, 0.0).astype(bf16) for h in range(HEADS)]
    return spread, plain


def live_rows(lengths, count):
    row = lax.broadcasted_iota(jnp.int32, (BLOCK, 1), 0)
    live = [jnp.where(row < lengths[b], 1.0, 0.0) for b in range(count // BLOCK)]
    return jnp.concatenate(live, axis=0) > 0.5


def attend_kernel(
    hops, rows, me, lengths, tokens, packed, other, cos, sin, weights, w_attn, gains, normed, heads, shares, mixture
):
    order = slot_order(hops, rows, me[0], 1)
    ordered = mm(order[:, : D // 2], packed[...]) + mm(order[:, D // 2 :], other[...])
    weights[...] = ordered[:, :QKV].astype(bf16)
    w_attn[...] = ordered[:, QKV : QKV + D].astype(bf16)
    here = lax.broadcasted_iota(jnp.int32, (D, D), 0) == lax.broadcasted_iota(jnp.int32, (D, D), 1)
    for k in range(2):
        column = ordered[:, QKV + D + k : QKV + D + k + 1]
        gains[k : k + 1, :] = jnp.sum(jnp.where(here, column, 0.0), axis=0, keepdims=True)
    gain = gains[0:1, :]
    w_qkv = weights[...]
    c, s = cos[...], sin[...]
    spread_masks, plain_masks = head_masks()
    key_lane = lax.broadcasted_iota(jnp.int32, (1, BLOCK), 1)
    count = tokens.shape[0] // BLOCK
    for part in [slice(b * BLOCK, (b + 1) * BLOCK) for b in range(count)]:
        normed[part] = (standardize(tokens[part].astype(f32))[0] * gain).astype(bf16)

    def rope(base):
        both = mm(normed[...], w_qkv[:, base : base + D])
        low, high = both[:, :HALF].reshape(count, BLOCK, HALF), both[:, HALF:].reshape(count, BLOCK, HALF)
        both = jnp.concatenate([low * c - high * s, high * c + low * s], axis=2)
        return both.reshape(count * BLOCK, D)

    heads[:, :D] = (rope(0) * HEAD_DIM ** (-0.5)).astype(bf16)
    heads[:, D : 2 * D] = rope(D).astype(bf16)
    heads[:, 2 * D :] = mm(normed[...], w_qkv[:, 2 * D :]).astype(bf16)
    parts = [slice(b * BLOCK, (b + 1) * BLOCK) for b in range(count)]
    for block in parts:
        shares[block] = mm_nt(heads[block, :D], stack_heads(heads[block, D : 2 * D], spread_masks))
    for b, block in enumerate(parts):
        live = key_lane < lengths[b]
        for h in range(HEADS):
            cut = slice(h * BLOCK, (h + 1) * BLOCK)
            one = jnp.where(live, shares[block, cut], -1e30)
            grown = jnp.exp(one - jnp.max(one, axis=1, keepdims=True))
            shares[block, cut] = grown * (1.0 / jnp.sum(grown, axis=1, keepdims=True))
    for block in parts:
        mixed = mm(shares[block].astype(bf16), stack_heads(heads[block, 2 * D :], plain_masks))
        mixture[block] = mixed.astype(bf16)


def feed_kernel(
    hops, rows, me, lengths, tokens, cot, packed, other, attn, gains, mixture,
    w_mlp, middle, hidden, d_middle, d_mixture, g_attn, sums, hat_two_low, out_low, d_att, d_merged,
):
    order = slot_order(hops, rows, me[0], 1)
    ordered = mm(order[:, : D // 2], packed[...]) + mm(order[:, D // 2 :], other[...])
    ordered = ordered.astype(bf16)
    w_attn = attn[...]
    w_in = ordered[:, : 2 * FF]
    w_mlp[...] = ordered[:, 2 * FF :]
    gain = gains[1:2, :]
    mid = tokens[...].astype(f32) + mm(mixture[...], w_attn)
    middle[...] = mid
    hat_two, inv_two = standardize(mid)
    hat_two_low[...] = (hat_two * gain).astype(bf16)
    merged = mm(hat_two_low[...], w_in)
    inner = merged[:, :FF]
    gate = merged[:, FF:]
    cdf = 0.5 * (1.0 + lax.erf(inner * 0.7071067811865476))
    curved = inner * cdf
    slope = cdf + inner * jnp.exp(-0.5 * inner * inner) * 0.3989422804014327
    hidden[...] = (curved * gate).astype(bf16)
    out_grad = jnp.where(live_rows(lengths, tokens.shape[0]), cot[...].astype(f32), 0.0)
    out_low[...] = out_grad.astype(bf16)
    d_hidden = mm(out_low[...], w_mlp[...])
    d_merged[:, :FF] = (d_hidden * gate * slope).astype(bf16)
    d_merged[:, FF:] = (d_hidden * curved).astype(bf16)
    d_normed = mm_nt(d_merged[...], w_in)
    d_mid = out_grad + norm_back(d_normed * gain, hat_two, inv_two)
    d_middle[...] = d_mid
    d_att[...] = d_mid.astype(bf16)
    d_mixture[...] = mm_nt(d_att[...], w_attn).astype(bf16)
    order = slot_order(hops, rows, me[0], 0)
    total = mm_tn(hat_two_low[...], d_merged[...]).astype(bf16)
    sums[:, : 2 * FF] = mm(order, total).astype(bf16)
    total = mm_tn(out_low[...], hidden[...]).astype(bf16)
    sums[:, 2 * FF :] = mm(order, total).astype(bf16)
    g_attn[...] = mm_tn(mixture[...], d_att[...]).astype(bf16)


def attend_back_kernel(
    hops, rows, me, heads, shares, d_mixture, normed, g_attn, cos, sin, sums, d_qkv
):
    c, s = cos[...], sin[...]
    spread_masks, plain_masks = head_masks()

    def rope_back(grads):
        low, high = grads[:, :HALF], grads[:, HALF:]
        return jnp.concatenate([low * c + high * s, high * c - low * s], axis=1).astype(bf16)

    parts = [slice(b * BLOCK, (b + 1) * BLOCK) for b in range(heads.shape[0] // BLOCK)]
    d_shares = [mm_nt(d_mixture[block], stack_heads(heads[block, 2 * D :], plain_masks)) for block in parts]
    d_values = [mm(turn_heads(shares[block].astype(bf16)), stack_heads(d_mixture[block], plain_masks)) for block in parts]
    for block, d_value in zip(parts, d_values):
        d_qkv[block, 2 * D :] = d_value.astype(bf16)
    d_scores = []
    for block, d_share in zip(parts, d_shares):
        pieces = []
        for h in range(HEADS):
            cut = slice(h * BLOCK, (h + 1) * BLOCK)
            one, d_one = shares[block, cut], d_share[:, cut]
            d_one = one * (d_one - jnp.sum(one * d_one, axis=1, keepdims=True))
            pieces.append(d_one.astype(bf16))
        d_scores.append(jnp.concatenate(pieces, axis=1))
    for block, d_score in zip(parts, d_scores):
        d_qkv[block, :D] = rope_back(mm(d_score, stack_heads(heads[block, D : 2 * D], spread_masks)) * HEAD_DIM ** (-0.5))
    for block, d_score in zip(parts, d_scores):
        d_qkv[block, D : 2 * D] = rope_back(mm(turn_heads(d_score), stack_heads(heads[block, :D], spread_masks)))
    order = slot_order(hops, rows, me[0], 0)
    total = mm_tn(normed[...], d_qkv[...]).astype(bf16)
    placed = mm(order, total).astype(bf16)
    spread = spread_columns(False)
    sums[:, :D] = mm(placed[:, :D], spread).astype(bf16)
    sums[:, D : 2 * D] = mm(placed[:, D : 2 * D], spread).astype(bf16)
    sums[:, 2 * D : QKV] = placed[:, 2 * D :]
    sums[:, QKV:] = mm(order, g_attn[...]).astype(bf16)


def outputs_kernel(lengths, tokens, weights, gains, d_qkv, d_middle, middle, hidden, w_mlp, out, grad):
    gain = gains[0:1, :]
    result = middle[...] + mm_nt(hidden[...], w_mlp[...])
    out[...] = jnp.where(live_rows(lengths, tokens.shape[0]), result, 0.0).astype(bf16)
    hat_one, inv_one = standardize(tokens[...].astype(f32))
    d_normed = mm_nt(d_qkv[...], weights[...])
    grad[...] = d_middle[...] + norm_back(d_normed * gain, hat_one, inv_one)


SMALL = pl.BlockSpec(memory_space=pltpu.SMEM)
NEAR = pl.BlockSpec(memory_space=pltpu.VMEM)


def call(kernel, in_specs, shapes, scratch=()):
    return pl.pallas_call(
        kernel,
        in_specs=in_specs,
        out_specs=[NEAR] * len(shapes),
        out_shape=[jax.ShapeDtypeStruct(shape, kind) for shape, kind in shapes],
        scratch_shapes=[pltpu.VMEM(shape, kind) for shape, kind in scratch],
        compiler_params=pltpu.CompilerParams(vmem_limit_bytes=32 * 1024 * 1024),
    )


def put(room, piece, slot, column=0):
    return lax.dynamic_update_slice(room, piece, (slot, 0, column))


def on_device(n, tokens, lengths, w_qkv, w_attn, w_in, w_mlp, gain_attn, gain_mlp, cotangent):
    rows = D // n
    count = tokens.shape[0]
    hops = []
    while 2 ** len(hops) < n:
        hops.append(n >> (len(hops) + 1))
    hops = tuple(hops)
    last = len(hops) - 1
    single = max(last - 2, 0)
    plane = [0]
    for mask in hops[single:last]:
        plane += [mask ^ other for other in plane]
    plane = plane[1:]
    size = 2**single
    gain_attn = gain_attn.reshape(1, rows)
    gain_mlp = gain_mlp.reshape(1, rows)

    def trade(values, mask):
        return lax.ppermute(values, "dp", [(i, i ^ mask) for i in range(n)])

    held = pl.pallas_call(
        pack_kernel, out_specs=NEAR, out_shape=jax.ShapeDtypeStruct((rows, FIRST + SECOND), bf16)
    )(w_qkv, w_attn, w_in, w_mlp.T, gain_attn, gain_mlp)
    room = put(jnp.zeros((size, rows, FIRST + SECOND), bf16), held[None], 0)
    for k in range(single):
        room = put(room, trade(room[: 2**k], hops[k]), 2**k)
    got = [trade(room, mask) for mask in plane]
    room = put(jnp.zeros((n // 2, rows, FIRST + SECOND), bf16), room, 0)
    for k, piece in enumerate(got):
        room = put(room, piece, size * (k + 1))
    first, second = room[:, :, :FIRST], room[:, :, FIRST:]
    first_got, second_got = trade(first, 1), trade(second, 1)
    first = first.reshape(D // 2, FIRST), first_got.reshape(D // 2, FIRST)
    second = second.reshape(D // 2, SECOND), second_got.reshape(D // 2, SECOND)

    cos, sin = tables()
    cos, sin = jnp.asarray(cos), jnp.asarray(sin)
    me = lax.axis_index("dp").astype(jnp.int32).reshape(1)
    weights, attn, gains, normed, heads, shares, mixture = call(
        functools.partial(attend_kernel, hops, rows),
        [SMALL] * 2 + [NEAR] * 5,
        [((D, QKV), bf16), ((D, D), bf16), ((2, D), f32), ((count, D), bf16), ((count, QKV), bf16), ((count, WIDE), f32), ((count, D), bf16)],
    )(me, lengths, tokens, *first, cos, sin)
    w_mlp_all, middle, hidden, d_middle, d_mixture, g_attn, second_sums = call(
        functools.partial(feed_kernel, hops, rows),
        [SMALL] * 2 + [NEAR] * 7,
        [((D, FF), bf16), ((count, D), f32), ((count, FF), bf16), ((count, D), f32), ((count, D), bf16), ((D, D), bf16), ((D, 3 * FF), bf16)],
        [((count, D), bf16), ((count, D), bf16), ((count, D), bf16), ((count, 2 * FF), bf16)],
    )(me, lengths, tokens, cotangent, *second, attn, gains, mixture)
    first_sums, d_qkv = call(
        functools.partial(attend_back_kernel, hops, rows),
        [SMALL] + [NEAR] * 7,
        [((D, SUMS), bf16), ((count, QKV), bf16)],
    )(me, heads, shares, d_mixture, normed, g_attn, cos, sin)
    out, grad = call(
        outputs_kernel, [SMALL] + [NEAR] * 8, [((count, D), bf16), ((count, D), f32)]
    )(lengths, tokens, weights, gains, d_qkv, d_middle, middle, hidden, w_mlp_all)

    def halve(kept, mask):
        half = kept.shape[0] // 2
        got = trade(kept[half:], mask)
        return (kept[:half].astype(f32) + got.astype(f32)).astype(bf16)

    first, second = first_sums.reshape(n, rows, SUMS), second_sums.reshape(n, rows, 3 * FF)
    first, second = halve(first, 1), halve(second, 1)
    kept = put(put(jnp.zeros((n // 2, rows, SUMS + 3 * FF), bf16), first, 0), second, 0, SUMS)
    got = [trade(kept[size * (k + 1) : size * (k + 2)], mask) for k, mask in enumerate(plane)]
    total = kept[:size].astype(f32)
    for piece in got:
        total = total + piece.astype(f32)
    kept = total.astype(bf16)
    for k in range(single - 1, 0, -1):
        kept = halve(kept, hops[k])
    got = trade(kept[1], hops[0])
    g_qkv, g_attn, g_in, g_mlp, g_first, g_second = call(
        end_kernel,
        [NEAR] * 6,
        [((rows, QKV), f32), ((rows, D), f32), ((rows, 2 * FF), f32), ((rows, FF), f32), ((1, rows), f32), ((1, rows), f32)],
    )(kept[0], got, w_qkv, w_in, gain_attn, gain_mlp)
    return out, grad, g_qkv, g_attn, g_in, g_mlp.T, g_first.reshape(rows), g_second.reshape(rows)


def solution(mesh):
    rows = P("dp", None)
    return jax.shard_map(
        functools.partial(on_device, mesh.shape["dp"]),
        mesh=mesh,
        in_specs=(rows, P("dp"), rows, rows, rows, P(None, "dp"), P("dp"), P("dp"), rows),
        out_specs=(rows, rows, rows, rows, rows, P(None, "dp"), P("dp"), P("dp")),
        check_vma=False,
    )
```

```python
import functools

import jax
import jax.numpy as jnp
import numpy as np
from jax import lax
from jax.experimental import pallas as pl
from jax.experimental.pallas import tpu as pltpu
from jax.sharding import PartitionSpec as P

D = 256
FF = 384
HEADS = 4
HEAD_DIM = 64
BLOCK = 128
HALF = D // 2
WIDE = HEADS * BLOCK
QKV = 3 * D
LANES = 128
FIRST = QKV + D + LANES
SECOND = 2 * FF + FF
SUMS = QKV + D

rope_base = 160000.0
eps_norm = 1e-05
bf16 = jnp.bfloat16
f32 = jnp.float32


def tables():
    half_dim = HEAD_DIM // 2
    frequency = rope_base ** (-(np.arange(half_dim) * 2.0) / HEAD_DIM)
    angles = np.arange(BLOCK)[:, None] * frequency[None, :]
    angles = np.tile(angles, (1, HEADS))
    return np.cos(angles).astype(np.float32), np.sin(angles).astype(np.float32)


def mm(left, right):
    return lax.dot_general(left, right, (((1,), (0,)), ((), ())), preferred_element_type=f32)


def mm_nt(left, right):
    return lax.dot_general(left, right, (((1,), (1,)), ((), ())), preferred_element_type=f32)


def mm_tn(left, right):
    return lax.dot_general(left, right, (((0,), (0,)), ((), ())), preferred_element_type=f32)


def spread_columns(forward):
    old = lax.broadcasted_iota(jnp.int32, (D, D), 0 if forward else 1)
    new = lax.broadcasted_iota(jnp.int32, (D, D), 1 if forward else 0)
    target = ((old // 32) % 2) * HALF + (old // HEAD_DIM) * 32 + old % 32
    return jnp.where(target == new, 1.0, 0.0).astype(bf16)


def to_column(row):
    size = row.shape[1]
    here = lax.broadcasted_iota(jnp.int32, (size, size), 0)
    there = lax.broadcasted_iota(jnp.int32, (size, size), 1)
    return jnp.sum(jnp.where(here == there, row, 0.0), axis=1, keepdims=True)


def to_row(column):
    size = column.shape[0]
    here = lax.broadcasted_iota(jnp.int32, (size, size), 0)
    there = lax.broadcasted_iota(jnp.int32, (size, size), 1)
    return jnp.sum(jnp.where(here == there, column, 0.0), axis=0, keepdims=True)


def pack_kernel(w_qkv, w_attn, w_in, w_mlp, gain_attn, gain_mlp, out):
    spread = spread_columns(True)
    out[:, :D] = mm(w_qkv[:, :D], spread).astype(bf16)
    out[:, D : 2 * D] = mm(w_qkv[:, D : 2 * D], spread).astype(bf16)
    out[:, 2 * D : QKV] = w_qkv[:, 2 * D :]
    out[:, QKV : QKV + D] = w_attn[...]
    lane = lax.broadcasted_iota(jnp.int32, (out.shape[0], LANES), 1)
    gains = jnp.where(lane == 0, to_column(gain_attn[...].astype(f32)), 0.0)
    gains = jnp.where(lane == 1, to_column(gain_mlp[...].astype(f32)), gains)
    out[:, QKV + D : FIRST] = gains.astype(bf16)
    out[:, FIRST : FIRST + 2 * FF] = w_in[...]
    out[:, FIRST + 2 * FF :] = w_mlp[...]


def end_kernel(*refs):
    w_qkv, w_in, gain_attn, gain_mlp, g_qkv, g_attn, g_in, g_mlp, g_first, g_second = refs[-10:]
    total = refs[0][...].astype(f32)
    for got in refs[1:-10]:
        total = total + got[...].astype(f32)
    part = total[:, :QKV]
    g_qkv[...] = part
    g_first[...] = to_row(jnp.sum(part * w_qkv[...].astype(f32), axis=1, keepdims=True)) / gain_attn[...].astype(f32)
    g_attn[...] = total[:, QKV : QKV + D]
    part = total[:, QKV + D : QKV + D + 2 * FF]
    g_in[...] = part
    g_second[...] = to_row(jnp.sum(part * w_in[...].astype(f32), axis=1, keepdims=True)) / gain_mlp[...].astype(f32)
    g_mlp[...] = total[:, QKV + D + 2 * FF :]


def standardize(values):
    centre = values - jnp.mean(values, axis=-1, keepdims=True)
    inverse = lax.rsqrt(jnp.mean(centre * centre, axis=-1, keepdims=True) + eps_norm)
    return centre * inverse, inverse


def norm_back(d_hat, hat_rows, inverse):
    mean_one = jnp.mean(d_hat, axis=-1, keepdims=True)
    mean_two = jnp.mean(d_hat * hat_rows, axis=-1, keepdims=True)
    return inverse * (d_hat - mean_one - hat_rows * mean_two)


def stack_heads(rows, masks):
    return jnp.concatenate([rows * mask for mask in masks], axis=0)


def turn_heads(values):
    return jnp.concatenate(
        [values[:, h * BLOCK : (h + 1) * BLOCK].T for h in range(HEADS)], axis=1
    )


def slot_order(hops, rows, me, slot_axis):
    slots = lax.broadcasted_iota(jnp.int32, (D, D), slot_axis)
    place = slots // rows
    owner = jnp.full((D, D), me, jnp.int32)
    for bit, mask in enumerate(hops):
        owner = owner ^ (((place >> bit) & 1) * mask)
    found = owner * rows + slots % rows == lax.broadcasted_iota(jnp.int32, (D, D), 1 - slot_axis)
    return jnp.where(found, 1.0, 0.0).astype(bf16)


def head_masks():
    lane = lax.broadcasted_iota(jnp.int32, (1, D), 1)
    spread = [jnp.where((lane % HALF) // 32 == h, 1.0, 0.0).astype(bf16) for h in range(HEADS)]
    plain = [jnp.where(lane // HEAD_DIM == h, 1.0, 0.0).astype(bf16) for h in range(HEADS)]
    return spread, plain


def live_rows(lengths, count):
    row = lax.broadcasted_iota(jnp.int32, (BLOCK, 1), 0)
    live = [jnp.where(row < lengths[b], 1.0, 0.0) for b in range(count // BLOCK)]
    return jnp.concatenate(live, axis=0) > 0.5


def attend_kernel(
    hops, rows, me, lengths, tokens, packed, other, cos, sin, weights, w_attn, gains, normed, heads, shares, mixture
):
    order = slot_order(hops, rows, me[0], 1)
    ordered = mm(order[:, : D // 2], packed[...]) + mm(order[:, D // 2 :], other[...])
    weights[...] = ordered[:, :QKV].astype(bf16)
    w_attn[...] = ordered[:, QKV : QKV + D].astype(bf16)
    here = lax.broadcasted_iota(jnp.int32, (D, D), 0) == lax.broadcasted_iota(jnp.int32, (D, D), 1)
    for k in range(2):
        column = ordered[:, QKV + D + k : QKV + D + k + 1]
        gains[k : k + 1, :] = jnp.sum(jnp.where(here, column, 0.0), axis=0, keepdims=True)
    gain = gains[0:1, :]
    w_qkv = weights[...]
    c, s = cos[...], sin[...]
    spread_masks, plain_masks = head_masks()
    key_lane = lax.broadcasted_iota(jnp.int32, (1, BLOCK), 1)
    count = tokens.shape[0] // BLOCK
    for part in [slice(b * BLOCK, (b + 1) * BLOCK) for b in range(count)]:
        normed[part] = (standardize(tokens[part].astype(f32))[0] * gain).astype(bf16)

    def rope(base):
        both = mm(normed[...], w_qkv[:, base : base + D])
        low, high = both[:, :HALF].reshape(count, BLOCK, HALF), both[:, HALF:].reshape(count, BLOCK, HALF)
        both = jnp.concatenate([low * c - high * s, high * c + low * s], axis=2)
        return both.reshape(count * BLOCK, D)

    heads[:, :D] = (rope(0) * HEAD_DIM ** (-0.5)).astype(bf16)
    heads[:, D : 2 * D] = rope(D).astype(bf16)
    heads[:, 2 * D :] = mm(normed[...], w_qkv[:, 2 * D :]).astype(bf16)
    parts = [slice(b * BLOCK, (b + 1) * BLOCK) for b in range(count)]
    for block in parts:
        shares[block] = mm_nt(heads[block, :D], stack_heads(heads[block, D : 2 * D], spread_masks))
    for b, block in enumerate(parts):
        live = key_lane < lengths[b]
        for h in range(HEADS):
            cut = slice(h * BLOCK, (h + 1) * BLOCK)
            one = jnp.where(live, shares[block, cut], -1e30)
            grown = jnp.exp(one - jnp.max(one, axis=1, keepdims=True))
            shares[block, cut] = grown * (1.0 / jnp.sum(grown, axis=1, keepdims=True))
    for block in parts:
        mixed = mm(shares[block].astype(bf16), stack_heads(heads[block, 2 * D :], plain_masks))
        mixture[block] = mixed.astype(bf16)


def feed_kernel(
    hops, rows, me, lengths, tokens, cot, packed, other, attn, gains, mixture,
    w_mlp, middle, hidden, d_middle, d_mixture, g_attn, sums, hat_two_low, out_low, d_att, d_merged,
):
    order = slot_order(hops, rows, me[0], 1)
    ordered = mm(order[:, : D // 2], packed[...]) + mm(order[:, D // 2 :], other[...])
    ordered = ordered.astype(bf16)
    w_attn = attn[...]
    w_in = ordered[:, : 2 * FF]
    w_mlp[...] = ordered[:, 2 * FF :]
    gain = gains[1:2, :]
    mid = tokens[...].astype(f32) + mm(mixture[...], w_attn)
    middle[...] = mid
    hat_two, inv_two = standardize(mid)
    hat_two_low[...] = (hat_two * gain).astype(bf16)
    merged = mm(hat_two_low[...], w_in)
    inner = merged[:, :FF]
    gate = merged[:, FF:]
    cdf = 0.5 * (1.0 + lax.erf(inner * 0.7071067811865476))
    curved = inner * cdf
    slope = cdf + inner * jnp.exp(-0.5 * inner * inner) * 0.3989422804014327
    hidden[...] = (curved * gate).astype(bf16)
    out_grad = jnp.where(live_rows(lengths, tokens.shape[0]), cot[...].astype(f32), 0.0)
    out_low[...] = out_grad.astype(bf16)
    d_hidden = mm(out_low[...], w_mlp[...])
    d_merged[:, :FF] = (d_hidden * gate * slope).astype(bf16)
    d_merged[:, FF:] = (d_hidden * curved).astype(bf16)
    d_normed = mm_nt(d_merged[...], w_in)
    d_mid = out_grad + norm_back(d_normed * gain, hat_two, inv_two)
    d_middle[...] = d_mid
    d_att[...] = d_mid.astype(bf16)
    d_mixture[...] = mm_nt(d_att[...], w_attn).astype(bf16)
    order = slot_order(hops, rows, me[0], 0)
    total = mm_tn(hat_two_low[...], d_merged[...]).astype(bf16)
    sums[:, : 2 * FF] = mm(order, total).astype(bf16)
    total = mm_tn(out_low[...], hidden[...]).astype(bf16)
    sums[:, 2 * FF :] = mm(order, total).astype(bf16)
    g_attn[...] = mm_tn(mixture[...], d_att[...]).astype(bf16)


def attend_back_kernel(
    hops, rows, me, heads, shares, d_mixture, normed, g_attn, cos, sin, sums, d_qkv
):
    c, s = cos[...], sin[...]
    spread_masks, plain_masks = head_masks()

    def rope_back(grads):
        low, high = grads[:, :HALF], grads[:, HALF:]
        return jnp.concatenate([low * c + high * s, high * c - low * s], axis=1).astype(bf16)

    parts = [slice(b * BLOCK, (b + 1) * BLOCK) for b in range(heads.shape[0] // BLOCK)]
    d_shares = [mm_nt(d_mixture[block], stack_heads(heads[block, 2 * D :], plain_masks)) for block in parts]
    d_values = [mm(turn_heads(shares[block].astype(bf16)), stack_heads(d_mixture[block], plain_masks)) for block in parts]
    for block, d_value in zip(parts, d_values):
        d_qkv[block, 2 * D :] = d_value.astype(bf16)
    d_scores = []
    for block, d_share in zip(parts, d_shares):
        pieces = []
        for h in range(HEADS):
            cut = slice(h * BLOCK, (h + 1) * BLOCK)
            one, d_one = shares[block, cut], d_share[:, cut]
            d_one = one * (d_one - jnp.sum(one * d_one, axis=1, keepdims=True))
            pieces.append(d_one.astype(bf16))
        d_scores.append(jnp.concatenate(pieces, axis=1))
    for block, d_score in zip(parts, d_scores):
        d_qkv[block, :D] = rope_back(mm(d_score, stack_heads(heads[block, D : 2 * D], spread_masks)) * HEAD_DIM ** (-0.5))
    for block, d_score in zip(parts, d_scores):
        d_qkv[block, D : 2 * D] = rope_back(mm(turn_heads(d_score), stack_heads(heads[block, :D], spread_masks)))
    order = slot_order(hops, rows, me[0], 0)
    total = mm_tn(normed[...], d_qkv[...]).astype(bf16)
    placed = mm(order, total).astype(bf16)
    spread = spread_columns(False)
    sums[:, :D] = mm(placed[:, :D], spread).astype(bf16)
    sums[:, D : 2 * D] = mm(placed[:, D : 2 * D], spread).astype(bf16)
    sums[:, 2 * D : QKV] = placed[:, 2 * D :]
    sums[:, QKV:] = mm(order, g_attn[...]).astype(bf16)


def outputs_kernel(lengths, tokens, weights, gains, d_qkv, d_middle, middle, hidden, w_mlp, out, grad):
    gain = gains[0:1, :]
    result = middle[...] + mm_nt(hidden[...], w_mlp[...])
    out[...] = jnp.where(live_rows(lengths, tokens.shape[0]), result, 0.0).astype(bf16)
    hat_one, inv_one = standardize(tokens[...].astype(f32))
    d_normed = mm_nt(d_qkv[...], weights[...])
    grad[...] = d_middle[...] + norm_back(d_normed * gain, hat_one, inv_one)


SMALL = pl.BlockSpec(memory_space=pltpu.SMEM)
NEAR = pl.BlockSpec(memory_space=pltpu.VMEM)


def call(kernel, in_specs, shapes, scratch=()):
    return pl.pallas_call(
        kernel,
        in_specs=in_specs,
        out_specs=[NEAR] * len(shapes),
        out_shape=[jax.ShapeDtypeStruct(shape, kind) for shape, kind in shapes],
        scratch_shapes=[pltpu.VMEM(shape, kind) for shape, kind in scratch],
        compiler_params=pltpu.CompilerParams(vmem_limit_bytes=32 * 1024 * 1024),
    )


def put(room, piece, slot, column=0):
    return lax.dynamic_update_slice(room, piece, (slot, 0, column))


def on_device(n, tokens, lengths, w_qkv, w_attn, w_in, w_mlp, gain_attn, gain_mlp, cotangent):
    rows = D // n
    count = tokens.shape[0]
    hops = []
    while 2 ** len(hops) < n:
        hops.append(n >> (len(hops) + 1))
    hops = tuple(hops)
    lead = hops[:-1]
    rounds = []
    if len(lead) % 2:
        rounds.append(((lead[0], 1),))
    for k in range(len(lead) % 2, len(lead), 2):
        one, two = lead[k], lead[k + 1]
        rounds.append(((one ^ two, 3), (one, 1), (two, 2)))
    gain_attn = gain_attn.reshape(1, rows)
    gain_mlp = gain_mlp.reshape(1, rows)

    def trade(values, mask):
        return lax.ppermute(values, "dp", [(i, i ^ mask) for i in range(n)])

    held = pl.pallas_call(
        pack_kernel, out_specs=NEAR, out_shape=jax.ShapeDtypeStruct((rows, FIRST + SECOND), bf16)
    )(w_qkv, w_attn, w_in, w_mlp.T, gain_attn, gain_mlp)
    room = held[None]
    for partners in rounds:
        size = room.shape[0]
        got = [(trade(room, mask), place) for mask, place in partners]
        room = put(jnp.zeros((size * (len(got) + 1), rows, FIRST + SECOND), bf16), room, 0)
        for piece, place in got:
            room = put(room, piece, size * place)
    first, second = room[:, :, :FIRST], room[:, :, FIRST:]
    first_got, second_got = trade(first, 1), trade(second, 1)
    first = first.reshape(D // 2, FIRST), first_got.reshape(D // 2, FIRST)
    second = second.reshape(D // 2, SECOND), second_got.reshape(D // 2, SECOND)

    cos, sin = tables()
    cos, sin = jnp.asarray(cos), jnp.asarray(sin)
    me = lax.axis_index("dp").astype(jnp.int32).reshape(1)
    weights, attn, gains, normed, heads, shares, mixture = call(
        functools.partial(attend_kernel, hops, rows),
        [SMALL] * 2 + [NEAR] * 5,
        [((D, QKV), bf16), ((D, D), bf16), ((2, D), f32), ((count, D), bf16), ((count, QKV), bf16), ((count, WIDE), f32), ((count, D), bf16)],
    )(me, lengths, tokens, *first, cos, sin)
    w_mlp_all, middle, hidden, d_middle, d_mixture, g_attn, second_sums = call(
        functools.partial(feed_kernel, hops, rows),
        [SMALL] * 2 + [NEAR] * 7,
        [((D, FF), bf16), ((count, D), f32), ((count, FF), bf16), ((count, D), f32), ((count, D), bf16), ((D, D), bf16), ((D, 3 * FF), bf16)],
        [((count, D), bf16), ((count, D), bf16), ((count, D), bf16), ((count, 2 * FF), bf16)],
    )(me, lengths, tokens, cotangent, *second, attn, gains, mixture)
    first_sums, d_qkv = call(
        functools.partial(attend_back_kernel, hops, rows),
        [SMALL] + [NEAR] * 7,
        [((D, SUMS), bf16), ((count, QKV), bf16)],
    )(me, heads, shares, d_mixture, normed, g_attn, cos, sin)
    out, grad = call(
        outputs_kernel, [SMALL] + [NEAR] * 8, [((count, D), bf16), ((count, D), f32)]
    )(lengths, tokens, weights, gains, d_qkv, d_middle, middle, hidden, w_mlp_all)

    def halve(kept, mask):
        half = kept.shape[0] // 2
        got = trade(kept[half:], mask)
        return (kept[:half].astype(f32) + got.astype(f32)).astype(bf16)

    first, second = first_sums.reshape(n, rows, SUMS), second_sums.reshape(n, rows, 3 * FF)
    first, second = halve(first, 1), halve(second, 1)
    kept = put(put(jnp.zeros((n // 2, rows, SUMS + 3 * FF), bf16), first, 0), second, 0, SUMS)
    for k, partners in enumerate(rounds[::-1]):
        size = kept.shape[0] // (len(partners) + 1)
        got = [trade(kept[size * place : size * (place + 1)], mask) for mask, place in partners]
        if k == len(rounds) - 1:
            break
        total = kept[:size].astype(f32)
        for piece in got:
            total = total + piece.astype(f32)
        kept = total.astype(bf16)
        if k == 0:
            kept, out, grad = lax.optimization_barrier((kept, out, grad))
    g_qkv, g_attn, g_in, g_mlp, g_first, g_second = call(
        end_kernel,
        [NEAR] * (5 + len(got)),
        [((rows, QKV), f32), ((rows, D), f32), ((rows, 2 * FF), f32), ((rows, FF), f32), ((1, rows), f32), ((1, rows), f32)],
    )(kept[0], *[piece[0] for piece in got], w_qkv, w_in, gain_attn, gain_mlp)
    return out, grad, g_qkv, g_attn, g_in, g_mlp.T, g_first.reshape(rows), g_second.reshape(rows)


def solution(mesh):
    rows = P("dp", None)
    return jax.shard_map(
        functools.partial(on_device, mesh.shape["dp"]),
        mesh=mesh,
        in_specs=(rows, P("dp"), rows, rows, rows, P(None, "dp"), P("dp"), P("dp"), rows),
        out_specs=(rows, rows, rows, rows, rows, P(None, "dp"), P("dp"), P("dp")),
        check_vma=False,
    )
```

```python
import functools

import jax
import jax.numpy as jnp
import numpy as np
from jax import lax
from jax.experimental import pallas as pl
from jax.experimental.pallas import tpu as pltpu
from jax.sharding import PartitionSpec as P

D = 256
FF = 384
HEADS = 4
HEAD_DIM = 64
BLOCK = 128
HALF = D // 2
WIDE = HEADS * BLOCK
QKV = 3 * D
LANES = 128
FIRST = QKV + D + LANES
SECOND = 2 * FF + FF
SUMS = QKV + D

rope_base = 160000.0
eps_norm = 1e-05
bf16 = jnp.bfloat16
f32 = jnp.float32


def tables():
    half_dim = HEAD_DIM // 2
    frequency = rope_base ** (-(np.arange(half_dim) * 2.0) / HEAD_DIM)
    angles = np.arange(BLOCK)[:, None] * frequency[None, :]
    angles = np.tile(angles, (1, HEADS))
    return np.cos(angles).astype(np.float32), np.sin(angles).astype(np.float32)


def mm(left, right):
    return lax.dot_general(left, right, (((1,), (0,)), ((), ())), preferred_element_type=f32)


def mm_nt(left, right):
    return lax.dot_general(left, right, (((1,), (1,)), ((), ())), preferred_element_type=f32)


def mm_tn(left, right):
    return lax.dot_general(left, right, (((0,), (0,)), ((), ())), preferred_element_type=f32)


def spread_columns(forward):
    old = lax.broadcasted_iota(jnp.int32, (D, D), 0 if forward else 1)
    new = lax.broadcasted_iota(jnp.int32, (D, D), 1 if forward else 0)
    target = ((old // 32) % 2) * HALF + (old // HEAD_DIM) * 32 + old % 32
    return jnp.where(target == new, 1.0, 0.0).astype(bf16)


def to_column(row):
    size = row.shape[1]
    here = lax.broadcasted_iota(jnp.int32, (size, size), 0)
    there = lax.broadcasted_iota(jnp.int32, (size, size), 1)
    return jnp.sum(jnp.where(here == there, row, 0.0), axis=1, keepdims=True)


def to_row(column):
    size = column.shape[0]
    here = lax.broadcasted_iota(jnp.int32, (size, size), 0)
    there = lax.broadcasted_iota(jnp.int32, (size, size), 1)
    return jnp.sum(jnp.where(here == there, column, 0.0), axis=0, keepdims=True)


def pack_kernel(w_qkv, w_attn, w_in, w_mlp, gain_attn, gain_mlp, out):
    spread = spread_columns(True)
    out[:, :D] = mm(w_qkv[:, :D], spread).astype(bf16)
    out[:, D : 2 * D] = mm(w_qkv[:, D : 2 * D], spread).astype(bf16)
    out[:, 2 * D : QKV] = w_qkv[:, 2 * D :]
    out[:, QKV : QKV + D] = w_attn[...]
    lane = lax.broadcasted_iota(jnp.int32, (out.shape[0], LANES), 1)
    gains = jnp.where(lane == 0, to_column(gain_attn[...].astype(f32)), 0.0)
    gains = jnp.where(lane == 1, to_column(gain_mlp[...].astype(f32)), gains)
    out[:, QKV + D : FIRST] = gains.astype(bf16)
    out[:, FIRST : FIRST + 2 * FF] = w_in[...]
    out[:, FIRST + 2 * FF :] = w_mlp[...]


def end_kernel(*refs):
    w_qkv, w_in, gain_attn, gain_mlp, g_qkv, g_attn, g_in, g_mlp, g_first, g_second = refs[-10:]
    total = refs[0][...].astype(f32)
    for got in refs[1:-10]:
        total = total + got[...].astype(f32)
    part = total[:, :QKV]
    g_qkv[...] = part
    g_first[...] = to_row(jnp.sum(part * w_qkv[...].astype(f32), axis=1, keepdims=True)) / gain_attn[...].astype(f32)
    g_attn[...] = total[:, QKV : QKV + D]
    part = total[:, QKV + D : QKV + D + 2 * FF]
    g_in[...] = part
    g_second[...] = to_row(jnp.sum(part * w_in[...].astype(f32), axis=1, keepdims=True)) / gain_mlp[...].astype(f32)
    g_mlp[...] = total[:, QKV + D + 2 * FF :]


def standardize(values):
    centre = values - jnp.mean(values, axis=-1, keepdims=True)
    inverse = lax.rsqrt(jnp.mean(centre * centre, axis=-1, keepdims=True) + eps_norm)
    return centre * inverse, inverse


def norm_back(d_hat, hat_rows, inverse):
    mean_one = jnp.mean(d_hat, axis=-1, keepdims=True)
    mean_two = jnp.mean(d_hat * hat_rows, axis=-1, keepdims=True)
    return inverse * (d_hat - mean_one - hat_rows * mean_two)


def stack_heads(rows, masks):
    return jnp.concatenate([rows * mask for mask in masks], axis=0)


def turn_heads(values):
    return jnp.concatenate(
        [values[:, h * BLOCK : (h + 1) * BLOCK].T for h in range(HEADS)], axis=1
    )


def head_masks():
    lane = lax.broadcasted_iota(jnp.int32, (1, D), 1)
    spread = [jnp.where((lane % HALF) // 32 == h, 1.0, 0.0).astype(bf16) for h in range(HEADS)]
    plain = [jnp.where(lane // HEAD_DIM == h, 1.0, 0.0).astype(bf16) for h in range(HEADS)]
    return spread, plain


def live_rows(lengths, count):
    row = lax.broadcasted_iota(jnp.int32, (BLOCK, 1), 0)
    live = [jnp.where(row < lengths[b], 1.0, 0.0) for b in range(count // BLOCK)]
    return jnp.concatenate(live, axis=0) > 0.5


def early_kernel(lengths, tokens, cot, hat, out_low):
    hat[...] = standardize(tokens[...].astype(f32))[0]
    live = live_rows(lengths, tokens.shape[0])
    out_low[...] = jnp.where(live, cot[...].astype(f32), 0.0).astype(bf16)


def attend_kernel(
    lengths, hat, packed, cos, sin, gains, normed, heads, shares, mixture
):
    w_qkv = packed[:, :QKV]
    here = lax.broadcasted_iota(jnp.int32, (D, D), 0) == lax.broadcasted_iota(jnp.int32, (D, D), 1)
    for k in range(2):
        column = packed[:, QKV + D + k : QKV + D + k + 1].astype(f32)
        gains[k : k + 1, :] = jnp.sum(jnp.where(here, column, 0.0), axis=0, keepdims=True)
    gain = gains[0:1, :]
    c, s = cos[...], sin[...]
    spread_masks, plain_masks = head_masks()
    key_lane = lax.broadcasted_iota(jnp.int32, (1, BLOCK), 1)
    count = hat.shape[0] // BLOCK
    for part in [slice(b * BLOCK, (b + 1) * BLOCK) for b in range(count)]:
        normed[part] = (hat[part] * gain).astype(bf16)

    def rope(base):
        both = mm(normed[...], w_qkv[:, base : base + D])
        low, high = both[:, :HALF].reshape(count, BLOCK, HALF), both[:, HALF:].reshape(count, BLOCK, HALF)
        both = jnp.concatenate([low * c - high * s, high * c + low * s], axis=2)
        return both.reshape(count * BLOCK, D)

    heads[:, :D] = (rope(0) * HEAD_DIM ** (-0.5)).astype(bf16)
    heads[:, D : 2 * D] = rope(D).astype(bf16)
    heads[:, 2 * D :] = mm(normed[...], w_qkv[:, 2 * D :]).astype(bf16)
    parts = [slice(b * BLOCK, (b + 1) * BLOCK) for b in range(count)]
    for block in parts:
        shares[block] = mm_nt(heads[block, :D], stack_heads(heads[block, D : 2 * D], spread_masks))
    for b, block in enumerate(parts):
        live = key_lane < lengths[b]
        for h in range(HEADS):
            cut = slice(h * BLOCK, (h + 1) * BLOCK)
            one = jnp.where(live, shares[block, cut], -1e30)
            grown = jnp.exp(one - jnp.max(one, axis=1, keepdims=True))
            shares[block, cut] = grown * (1.0 / jnp.sum(grown, axis=1, keepdims=True))
    for block in parts:
        mixed = mm(shares[block].astype(bf16), stack_heads(heads[block, 2 * D :], plain_masks))
        mixture[block] = mixed.astype(bf16)


def feed_kernel(
    tokens, out_low, first, second, gains, mixture,
    middle, hidden, d_middle, d_mixture, g_attn, sums, hat_two_low, d_att, d_merged,
):
    w_attn = first[:, QKV : QKV + D]
    w_in = second[:, : 2 * FF]
    w_mlp = second[:, 2 * FF :]
    gain = gains[1:2, :]
    mid = tokens[...].astype(f32) + mm(mixture[...], w_attn)
    middle[...] = mid
    hat_two, inv_two = standardize(mid)
    hat_two_low[...] = (hat_two * gain).astype(bf16)
    merged = mm(hat_two_low[...], w_in)
    inner = merged[:, :FF]
    gate = merged[:, FF:]
    cdf = 0.5 * (1.0 + lax.erf(inner * 0.7071067811865476))
    curved = inner * cdf
    slope = cdf + inner * jnp.exp(-0.5 * inner * inner) * 0.3989422804014327
    hidden[...] = (curved * gate).astype(bf16)
    out_grad = out_low[...].astype(f32)
    d_hidden = mm(out_low[...], w_mlp)
    d_merged[:, :FF] = (d_hidden * gate * slope).astype(bf16)
    d_merged[:, FF:] = (d_hidden * curved).astype(bf16)
    d_normed = mm_nt(d_merged[...], w_in)
    d_mid = out_grad + norm_back(d_normed * gain, hat_two, inv_two)
    d_middle[...] = d_mid
    d_att[...] = d_mid.astype(bf16)
    d_mixture[...] = mm_nt(d_att[...], w_attn).astype(bf16)
    sums[:, : 2 * FF] = mm_tn(hat_two_low[...], d_merged[...]).astype(bf16)
    sums[:, 2 * FF :] = mm_tn(out_low[...], hidden[...]).astype(bf16)
    g_attn[...] = mm_tn(mixture[...], d_att[...]).astype(bf16)


def attend_back_kernel(
    heads, shares, d_mixture, normed, g_attn, cos, sin, sums, d_qkv
):
    c, s = cos[...], sin[...]
    spread_masks, plain_masks = head_masks()

    def rope_back(grads):
        low, high = grads[:, :HALF], grads[:, HALF:]
        return jnp.concatenate([low * c + high * s, high * c - low * s], axis=1).astype(bf16)

    parts = [slice(b * BLOCK, (b + 1) * BLOCK) for b in range(heads.shape[0] // BLOCK)]
    d_shares = [mm_nt(d_mixture[block], stack_heads(heads[block, 2 * D :], plain_masks)) for block in parts]
    d_values = [mm(turn_heads(shares[block].astype(bf16)), stack_heads(d_mixture[block], plain_masks)) for block in parts]
    for block, d_value in zip(parts, d_values):
        d_qkv[block, 2 * D :] = d_value.astype(bf16)
    d_scores = []
    for block, d_share in zip(parts, d_shares):
        pieces = []
        for h in range(HEADS):
            cut = slice(h * BLOCK, (h + 1) * BLOCK)
            one, d_one = shares[block, cut], d_share[:, cut]
            d_one = one * (d_one - jnp.sum(one * d_one, axis=1, keepdims=True))
            pieces.append(d_one.astype(bf16))
        d_scores.append(jnp.concatenate(pieces, axis=1))
    for block, d_score in zip(parts, d_scores):
        d_qkv[block, :D] = rope_back(mm(d_score, stack_heads(heads[block, D : 2 * D], spread_masks)) * HEAD_DIM ** (-0.5))
    for block, d_score in zip(parts, d_scores):
        d_qkv[block, D : 2 * D] = rope_back(mm(turn_heads(d_score), stack_heads(heads[block, :D], spread_masks)))
    total = mm_tn(normed[...], d_qkv[...]).astype(bf16)
    spread = spread_columns(False)
    sums[:, :D] = mm(total[:, :D], spread).astype(bf16)
    sums[:, D : 2 * D] = mm(total[:, D : 2 * D], spread).astype(bf16)
    sums[:, 2 * D : QKV] = total[:, 2 * D :]
    sums[:, QKV:] = g_attn[...]


def outputs_kernel(lengths, tokens, first, second, gains, d_qkv, d_middle, middle, hidden, out, grad):
    gain = gains[0:1, :]
    result = middle[...] + mm_nt(hidden[...], second[:, 2 * FF :])
    out[...] = jnp.where(live_rows(lengths, tokens.shape[0]), result, 0.0).astype(bf16)
    hat_one, inv_one = standardize(tokens[...].astype(f32))
    d_normed = mm_nt(d_qkv[...], first[:, :QKV])
    grad[...] = d_middle[...] + norm_back(d_normed * gain, hat_one, inv_one)


SMALL = pl.BlockSpec(memory_space=pltpu.SMEM)
NEAR = pl.BlockSpec(memory_space=pltpu.VMEM)


def call(kernel, in_specs, shapes, scratch=()):
    return pl.pallas_call(
        kernel,
        in_specs=in_specs,
        out_specs=[NEAR] * len(shapes),
        out_shape=[jax.ShapeDtypeStruct(shape, kind) for shape, kind in shapes],
        scratch_shapes=[pltpu.VMEM(shape, kind) for shape, kind in scratch],
        compiler_params=pltpu.CompilerParams(vmem_limit_bytes=32 * 1024 * 1024),
    )


def put(room, piece, place, column=0):
    return lax.dynamic_update_slice(room, piece[:, None], (0, place, 0, column))


def cut(room, place, ways):
    room = room.reshape(-1, ways, *room.shape[1:])
    return lax.dynamic_index_in_dim(room, place, 1, keepdims=False)


def on_device(n, tokens, lengths, w_qkv, w_attn, w_in, w_mlp, gain_attn, gain_mlp, cotangent):
    rows = D // n
    count = tokens.shape[0]
    hops = []
    while 2 ** len(hops) < n:
        hops.append(n >> (len(hops) + 1))
    hops = tuple(hops)
    lead = hops[:-1]
    me = lax.axis_index("dp")
    core = me & 1
    rounds = []
    if len(lead) % 2:
        rounds.append((me // lead[0], ((lead[0], 1),)))
    for k in range(len(lead) % 2, len(lead), 2):
        one, two = lead[k], lead[k + 1]
        rounds.append(((me // two) & 3, ((one ^ two, 3), (one, 2), (two, 1))))
    gain_attn = gain_attn.reshape(1, rows)
    gain_mlp = gain_mlp.reshape(1, rows)

    def trade(values, mask):
        return lax.ppermute(values, "dp", [(i, i ^ mask) for i in range(n)])

    held = pl.pallas_call(
        pack_kernel, out_specs=NEAR, out_shape=jax.ShapeDtypeStruct((rows, FIRST + SECOND), bf16)
    )(w_qkv, w_attn, w_in, w_mlp.T, gain_attn, gain_mlp)
    room = held[None]
    for place, partners in rounds:
        got = [(trade(room, mask), other) for mask, other in partners]
        wide = put(jnp.zeros((room.shape[0], len(got) + 1, rows, FIRST + SECOND), bf16), room, place)
        for piece, other in got:
            wide = put(wide, piece, place ^ other)
        room = wide.reshape(-1, rows, FIRST + SECOND)
        if place is rounds[0][0]:
            early = lax.optimization_barrier((room, tokens, cotangent))
            room = early[0]
            hat, out_low = call(
                early_kernel, [SMALL] + [NEAR] * 2, [((count, D), f32), ((count, D), bf16)]
            )(lengths, *early[1:])
    room, hat, out_low = lax.optimization_barrier((room, hat, out_low))

    def both(half):
        wide = put(jnp.zeros((n // 2, 2) + half.shape[1:], bf16), half, core)
        return put(wide, trade(half, 1), core ^ 1).reshape(D, half.shape[2])

    first, second = both(room[:, :, :FIRST]), both(room[:, :, FIRST:])

    cos, sin = tables()
    cos, sin = jnp.asarray(cos), jnp.asarray(sin)
    gains, normed, heads, shares, mixture = call(
        attend_kernel,
        [SMALL] + [NEAR] * 4,
        [((2, D), f32), ((count, D), bf16), ((count, QKV), bf16), ((count, WIDE), f32), ((count, D), bf16)],
    )(lengths, hat, first, cos, sin)
    middle, hidden, d_middle, d_mixture, g_attn, second_sums = call(
        feed_kernel,
        [NEAR] * 6,
        [((count, D), f32), ((count, FF), bf16), ((count, D), f32), ((count, D), bf16), ((D, D), bf16), ((D, 3 * FF), bf16)],
        [((count, D), bf16), ((count, D), bf16), ((count, 2 * FF), bf16)],
    )(tokens, out_low, first, second, gains, mixture)
    first_sums, d_qkv = call(
        attend_back_kernel, [NEAR] * 7, [((D, SUMS), bf16), ((count, QKV), bf16)]
    )(heads, shares, d_mixture, normed, g_attn, cos, sin)
    out, grad = call(
        outputs_kernel, [SMALL] + [NEAR] * 8, [((count, D), bf16), ((count, D), f32)]
    )(lengths, tokens, first, second, gains, d_qkv, d_middle, middle, hidden)

    def halve(sums):
        sums = sums.reshape(n, rows, sums.shape[1])
        got = trade(cut(sums, core ^ 1, 2), 1)
        return (cut(sums, core, 2).astype(f32) + got.astype(f32)).astype(bf16)

    kept = jnp.concatenate([halve(first_sums), halve(second_sums)], axis=2)
    for k, (place, partners) in enumerate(rounds[::-1]):
        ways = len(partners) + 1
        got = [trade(cut(kept, place ^ other, ways), mask) for mask, other in partners]
        kept = cut(kept, place, ways)
        if k == len(rounds) - 1:
            break
        total = kept.astype(f32)
        for piece in got:
            total = total + piece.astype(f32)
        kept = total.astype(bf16)
        if k == 0:
            kept, out, grad = lax.optimization_barrier((kept, out, grad))
    g_qkv, g_attn, g_in, g_mlp, g_first, g_second = call(
        end_kernel,
        [NEAR] * (5 + len(got)),
        [((rows, QKV), f32), ((rows, D), f32), ((rows, 2 * FF), f32), ((rows, FF), f32), ((1, rows), f32), ((1, rows), f32)],
    )(kept[0], *[piece[0] for piece in got], w_qkv, w_in, gain_attn, gain_mlp)
    return out, grad, g_qkv, g_attn, g_in, g_mlp.T, g_first.reshape(rows), g_second.reshape(rows)


def solution(mesh):
    rows = P("dp", None)
    return jax.shard_map(
        functools.partial(on_device, mesh.shape["dp"]),
        mesh=mesh,
        in_specs=(rows, P("dp"), rows, rows, rows, P(None, "dp"), P("dp"), P("dp"), rows),
        out_specs=(rows, rows, rows, rows, rows, P(None, "dp"), P("dp"), P("dp")),
        check_vma=False,
    )
```

```python
import functools

import jax
import jax.numpy as jnp
import numpy as np
from jax import lax
from jax.experimental import pallas as pl
from jax.experimental.pallas import tpu as pltpu
from jax.sharding import PartitionSpec as P

D = 256
FF = 384
HEADS = 4
HEAD_DIM = 64
BLOCK = 128
HALF = D // 2
WIDE = HEADS * BLOCK
QKV = 3 * D
LANES = 128
FIRST = QKV + D + LANES
SECOND = 2 * FF + FF
SUMS = QKV + D

rope_base = 160000.0
eps_norm = 1e-05
bf16 = jnp.bfloat16
f32 = jnp.float32


def tables():
    half_dim = HEAD_DIM // 2
    frequency = rope_base ** (-(np.arange(half_dim) * 2.0) / HEAD_DIM)
    angles = np.arange(BLOCK)[:, None] * frequency[None, :]
    angles = np.tile(angles, (1, HEADS))
    return np.cos(angles).astype(np.float32), np.sin(angles).astype(np.float32)


def mm(left, right):
    return lax.dot_general(left, right, (((1,), (0,)), ((), ())), preferred_element_type=f32)


def mm_nt(left, right):
    return lax.dot_general(left, right, (((1,), (1,)), ((), ())), preferred_element_type=f32)


def mm_tn(left, right):
    return lax.dot_general(left, right, (((0,), (0,)), ((), ())), preferred_element_type=f32)


def spread_columns(forward):
    old = lax.broadcasted_iota(jnp.int32, (D, D), 0 if forward else 1)
    new = lax.broadcasted_iota(jnp.int32, (D, D), 1 if forward else 0)
    target = ((old // 32) % 2) * HALF + (old // HEAD_DIM) * 32 + old % 32
    return jnp.where(target == new, 1.0, 0.0).astype(bf16)


def to_column(row):
    size = row.shape[1]
    here = lax.broadcasted_iota(jnp.int32, (size, size), 0)
    there = lax.broadcasted_iota(jnp.int32, (size, size), 1)
    return jnp.sum(jnp.where(here == there, row, 0.0), axis=1, keepdims=True)


def to_row(column):
    size = column.shape[0]
    here = lax.broadcasted_iota(jnp.int32, (size, size), 0)
    there = lax.broadcasted_iota(jnp.int32, (size, size), 1)
    return jnp.sum(jnp.where(here == there, column, 0.0), axis=0, keepdims=True)


def pack_kernel(w_qkv, w_attn, w_in, w_mlp, gain_attn, gain_mlp, out):
    spread = spread_columns(True)
    out[:, :D] = mm(w_qkv[:, :D], spread).astype(bf16)
    out[:, D : 2 * D] = mm(w_qkv[:, D : 2 * D], spread).astype(bf16)
    out[:, 2 * D : QKV] = w_qkv[:, 2 * D :]
    out[:, QKV : QKV + D] = w_attn[...]
    lane = lax.broadcasted_iota(jnp.int32, (out.shape[0], LANES), 1)
    gains = jnp.where(lane == 0, to_column(gain_attn[...].astype(f32)), 0.0)
    gains = jnp.where(lane == 1, to_column(gain_mlp[...].astype(f32)), gains)
    out[:, QKV + D : FIRST] = gains.astype(bf16)
    out[:, FIRST : FIRST + 2 * FF] = w_in[...]
    out[:, FIRST + 2 * FF :] = w_mlp[...]


def end_kernel(*refs):
    w_qkv, w_in, gain_attn, gain_mlp, g_qkv, g_attn, g_in, g_mlp, g_first, g_second = refs[-10:]
    total = refs[0][...].astype(f32)
    for got in refs[1:-10]:
        total = total + got[...].astype(f32)
    part = total[:, :QKV]
    g_qkv[...] = part
    g_first[...] = to_row(jnp.sum(part * w_qkv[...].astype(f32), axis=1, keepdims=True)) / gain_attn[...].astype(f32)
    g_attn[...] = total[:, QKV : QKV + D]
    part = total[:, QKV + D : QKV + D + 2 * FF]
    g_in[...] = part
    g_second[...] = to_row(jnp.sum(part * w_in[...].astype(f32), axis=1, keepdims=True)) / gain_mlp[...].astype(f32)
    g_mlp[...] = total[:, QKV + D + 2 * FF :]


def standardize(values):
    centre = values - jnp.mean(values, axis=-1, keepdims=True)
    inverse = lax.rsqrt(jnp.mean(centre * centre, axis=-1, keepdims=True) + eps_norm)
    return centre * inverse, inverse


def norm_back(d_hat, hat_rows, inverse):
    mean_one = jnp.mean(d_hat, axis=-1, keepdims=True)
    mean_two = jnp.mean(d_hat * hat_rows, axis=-1, keepdims=True)
    return inverse * (d_hat - mean_one - hat_rows * mean_two)


def stack_heads(rows, masks):
    return jnp.concatenate([rows * mask for mask in masks], axis=0)


def turn_heads(values):
    return jnp.concatenate(
        [values[:, h * BLOCK : (h + 1) * BLOCK].T for h in range(HEADS)], axis=1
    )


def head_masks():
    lane = lax.broadcasted_iota(jnp.int32, (1, D), 1)
    spread = [jnp.where((lane % HALF) // 32 == h, 1.0, 0.0).astype(bf16) for h in range(HEADS)]
    plain = [jnp.where(lane // HEAD_DIM == h, 1.0, 0.0).astype(bf16) for h in range(HEADS)]
    return spread, plain


def live_rows(lengths, count):
    row = lax.broadcasted_iota(jnp.int32, (BLOCK, 1), 0)
    live = [jnp.where(row < lengths[b], 1.0, 0.0) for b in range(count // BLOCK)]
    return jnp.concatenate(live, axis=0) > 0.5


def early_kernel(lengths, tokens, cot, hat, out_low):
    hat[...] = standardize(tokens[...].astype(f32))[0]
    live = live_rows(lengths, tokens.shape[0])
    out_low[...] = jnp.where(live, cot[...].astype(f32), 0.0).astype(bf16)


def attend_kernel(
    lengths, hat, packed, cos, sin, gains, normed, heads, shares, mixture
):
    w_qkv = packed[:, :QKV]
    here = lax.broadcasted_iota(jnp.int32, (D, D), 0) == lax.broadcasted_iota(jnp.int32, (D, D), 1)
    for k in range(2):
        column = packed[:, QKV + D + k : QKV + D + k + 1].astype(f32)
        gains[k : k + 1, :] = jnp.sum(jnp.where(here, column, 0.0), axis=0, keepdims=True)
    gain = gains[0:1, :]
    c, s = cos[...], sin[...]
    spread_masks, plain_masks = head_masks()
    key_lane = lax.broadcasted_iota(jnp.int32, (1, BLOCK), 1)
    count = hat.shape[0] // BLOCK
    for part in [slice(b * BLOCK, (b + 1) * BLOCK) for b in range(count)]:
        normed[part] = (hat[part] * gain).astype(bf16)

    def rope(base):
        both = mm(normed[...], w_qkv[:, base : base + D])
        low, high = both[:, :HALF].reshape(count, BLOCK, HALF), both[:, HALF:].reshape(count, BLOCK, HALF)
        both = jnp.concatenate([low * c - high * s, high * c + low * s], axis=2)
        return both.reshape(count * BLOCK, D)

    heads[:, :D] = (rope(0) * HEAD_DIM ** (-0.5)).astype(bf16)
    heads[:, D : 2 * D] = rope(D).astype(bf16)
    heads[:, 2 * D :] = mm(normed[...], w_qkv[:, 2 * D :]).astype(bf16)
    parts = [slice(b * BLOCK, (b + 1) * BLOCK) for b in range(count)]
    for block in parts:
        shares[block] = mm_nt(heads[block, :D], stack_heads(heads[block, D : 2 * D], spread_masks))
    for b, block in enumerate(parts):
        live = key_lane < lengths[b]
        for h in range(HEADS):
            cut = slice(h * BLOCK, (h + 1) * BLOCK)
            one = jnp.where(live, shares[block, cut], -1e30)
            grown = jnp.exp(one - jnp.max(one, axis=1, keepdims=True))
            shares[block, cut] = grown * (1.0 / jnp.sum(grown, axis=1, keepdims=True))
    for block in parts:
        mixed = mm(shares[block].astype(bf16), stack_heads(heads[block, 2 * D :], plain_masks))
        mixture[block] = mixed.astype(bf16)


def middle_kernel(
    tokens, out_low, first, second, gains, mixture, heads, shares, normed, cos, sin,
    middle, hidden, d_middle, second_sums, first_sums, d_qkv, d_mixture, hat_two_low, d_att, d_merged,
):
    feed(
        tokens, out_low, first, second, gains, mixture,
        middle, hidden, d_middle, d_mixture, hat_two_low, d_att, d_merged,
    )
    second_sums[:, : 2 * FF] = mm_tn(hat_two_low[...], d_merged[...]).astype(bf16)
    second_sums[:, 2 * FF :] = mm_tn(out_low[...], hidden[...]).astype(bf16)
    attend_back(heads, shares, d_mixture, normed, mixture, d_att, cos, sin, first_sums, d_qkv)


def feed(
    tokens, out_low, first, second, gains, mixture,
    middle, hidden, d_middle, d_mixture, hat_two_low, d_att, d_merged,
):
    w_attn = first[:, QKV : QKV + D]
    w_in = second[:, : 2 * FF]
    w_mlp = second[:, 2 * FF :]
    gain = gains[1:2, :]
    mid = tokens[...].astype(f32) + mm(mixture[...], w_attn)
    middle[...] = mid
    hat_two, inv_two = standardize(mid)
    hat_two_low[...] = (hat_two * gain).astype(bf16)
    merged = mm(hat_two_low[...], w_in)
    inner = merged[:, :FF]
    gate = merged[:, FF:]
    cdf = 0.5 * (1.0 + lax.erf(inner * 0.7071067811865476))
    curved = inner * cdf
    slope = cdf + inner * jnp.exp(-0.5 * inner * inner) * 0.3989422804014327
    hidden[...] = (curved * gate).astype(bf16)
    out_grad = out_low[...].astype(f32)
    d_hidden = mm(out_low[...], w_mlp)
    d_merged[:, :FF] = (d_hidden * gate * slope).astype(bf16)
    d_merged[:, FF:] = (d_hidden * curved).astype(bf16)
    d_normed = mm_nt(d_merged[...], w_in)
    d_mid = out_grad + norm_back(d_normed * gain, hat_two, inv_two)
    d_middle[...] = d_mid
    d_att[...] = d_mid.astype(bf16)
    d_mixture[...] = mm_nt(d_att[...], w_attn).astype(bf16)


def attend_back(heads, shares, d_mixture, normed, mixture, d_att, cos, sin, sums, d_qkv):
    c, s = cos[...], sin[...]
    spread_masks, plain_masks = head_masks()

    def rope_back(grads):
        low, high = grads[:, :HALF], grads[:, HALF:]
        return jnp.concatenate([low * c + high * s, high * c - low * s], axis=1).astype(bf16)

    parts = [slice(b * BLOCK, (b + 1) * BLOCK) for b in range(heads.shape[0] // BLOCK)]
    d_shares = [mm_nt(d_mixture[block], stack_heads(heads[block, 2 * D :], plain_masks)) for block in parts]
    d_values = [mm(turn_heads(shares[block].astype(bf16)), stack_heads(d_mixture[block], plain_masks)) for block in parts]
    for block, d_value in zip(parts, d_values):
        d_qkv[block, 2 * D :] = d_value.astype(bf16)
    d_scores = []
    for block, d_share in zip(parts, d_shares):
        pieces = []
        for h in range(HEADS):
            cut = slice(h * BLOCK, (h + 1) * BLOCK)
            one, d_one = shares[block, cut], d_share[:, cut]
            d_one = one * (d_one - jnp.sum(one * d_one, axis=1, keepdims=True))
            pieces.append(d_one.astype(bf16))
        d_scores.append(jnp.concatenate(pieces, axis=1))
    for block, d_score in zip(parts, d_scores):
        d_qkv[block, :D] = rope_back(mm(d_score, stack_heads(heads[block, D : 2 * D], spread_masks)) * HEAD_DIM ** (-0.5))
    for block, d_score in zip(parts, d_scores):
        d_qkv[block, D : 2 * D] = rope_back(mm(turn_heads(d_score), stack_heads(heads[block, :D], spread_masks)))
    total = mm_tn(normed[...], d_qkv[...]).astype(bf16)
    spread = spread_columns(False)
    sums[:, :D] = mm(total[:, :D], spread).astype(bf16)
    sums[:, D : 2 * D] = mm(total[:, D : 2 * D], spread).astype(bf16)
    sums[:, 2 * D : QKV] = total[:, 2 * D :]
    sums[:, QKV:] = mm_tn(mixture[...], d_att[...]).astype(bf16)


def outputs_kernel(lengths, tokens, first, second, gains, d_qkv, d_middle, middle, hidden, out, grad):
    gain = gains[0:1, :]
    result = middle[...] + mm_nt(hidden[...], second[:, 2 * FF :])
    out[...] = jnp.where(live_rows(lengths, tokens.shape[0]), result, 0.0).astype(bf16)
    hat_one, inv_one = standardize(tokens[...].astype(f32))
    d_normed = mm_nt(d_qkv[...], first[:, :QKV])
    grad[...] = d_middle[...] + norm_back(d_normed * gain, hat_one, inv_one)


GATHER_LEAD, GATHER_LAST = (2, 3, 1), (1, 2, 3)
REDUCE_LEAD, REDUCE_LAST = (1, 2, 3), (3, 1, 2)
SMALL = pl.BlockSpec(memory_space=pltpu.SMEM)
NEAR = pl.BlockSpec(memory_space=pltpu.VMEM)


def call(kernel, in_specs, shapes, scratch=()):
    return pl.pallas_call(
        kernel,
        in_specs=in_specs,
        out_specs=[NEAR] * len(shapes),
        out_shape=[jax.ShapeDtypeStruct(shape, kind) for shape, kind in shapes],
        scratch_shapes=[pltpu.VMEM(shape, kind) for shape, kind in scratch],
        compiler_params=pltpu.CompilerParams(vmem_limit_bytes=32 * 1024 * 1024),
    )


def put(room, piece, place, column=0):
    return lax.dynamic_update_slice(room, piece[:, None], (0, place, 0, column))


def cut(room, place, ways):
    room = room.reshape(-1, ways, *room.shape[1:])
    return lax.dynamic_index_in_dim(room, place, 1, keepdims=False)


def on_device(n, tokens, lengths, w_qkv, w_attn, w_in, w_mlp, gain_attn, gain_mlp, cotangent):
    rows = D // n
    count = tokens.shape[0]
    hops = []
    while 2 ** len(hops) < n:
        hops.append(n >> (len(hops) + 1))
    hops = tuple(hops)
    lead = hops[:-1]
    me = lax.axis_index("dp")
    core = me & 1
    rounds = []
    if len(lead) % 2:
        rounds.append((me // lead[0], ((lead[0], 1),), ((lead[0], 1),)))
    for k in range(len(lead) % 2, len(lead), 2):
        one, two = lead[k], lead[k + 1]
        masks = {1: two, 2: one, 3: one ^ two}
        orders = (GATHER_LAST, REDUCE_LAST) if k + 2 == len(lead) else (GATHER_LEAD, REDUCE_LEAD)
        rounds.append(((me // two) & 3, *[tuple((masks[p], p) for p in order) for order in orders]))
    gain_attn = gain_attn.reshape(1, rows)
    gain_mlp = gain_mlp.reshape(1, rows)

    def trade(values, mask):
        return lax.ppermute(values, "dp", [(i, i ^ mask) for i in range(n)])

    held = pl.pallas_call(
        pack_kernel, out_specs=NEAR, out_shape=jax.ShapeDtypeStruct((rows, FIRST + SECOND), bf16)
    )(w_qkv, w_attn, w_in, w_mlp.T, gain_attn, gain_mlp)
    room = held[None]
    for place, partners, _ in rounds:
        got = [(trade(room, mask), other) for mask, other in partners]
        wide = put(jnp.zeros((room.shape[0], len(got) + 1, rows, FIRST + SECOND), bf16), room, place)
        for piece, other in got:
            wide = put(wide, piece, place ^ other)
        room = wide.reshape(-1, rows, FIRST + SECOND)
        if place is rounds[0][0]:
            early = lax.optimization_barrier((room, tokens, cotangent))
            room = early[0]
            hat, out_low = call(
                early_kernel, [SMALL] + [NEAR] * 2, [((count, D), f32), ((count, D), bf16)]
            )(lengths, *early[1:])
    room, hat, out_low = lax.optimization_barrier((room, hat, out_low))

    def both(half, got):
        wide = put(jnp.zeros((n // 2, 2) + half.shape[1:], bf16), half, core)
        return put(wide, got, core ^ 1).reshape(D, half.shape[2])

    first, second = room[:, :, :FIRST], room[:, :, FIRST:]
    got = trade(first, 1)
    got, second = lax.optimization_barrier((got, second))
    first, second = both(first, got), both(second, trade(second, 1))

    cos, sin = tables()
    cos, sin = jnp.asarray(cos), jnp.asarray(sin)
    gains, normed, heads, shares, mixture = call(
        attend_kernel,
        [SMALL] + [NEAR] * 4,
        [((2, D), f32), ((count, D), bf16), ((count, QKV), bf16), ((count, WIDE), f32), ((count, D), bf16)],
    )(lengths, hat, first, cos, sin)
    middle, hidden, d_middle, second_sums, first_sums, d_qkv = call(
        middle_kernel,
        [NEAR] * 11,
        [((count, D), f32), ((count, FF), bf16), ((count, D), f32), ((D, 3 * FF), bf16), ((D, SUMS), bf16), ((count, QKV), bf16)],
        [((count, D), bf16), ((count, D), bf16), ((count, D), bf16), ((count, 2 * FF), bf16)],
    )(tokens, out_low, first, second, gains, mixture, heads, shares, normed, cos, sin)
    out, grad = call(
        outputs_kernel, [SMALL] + [NEAR] * 8, [((count, D), bf16), ((count, D), f32)]
    )(lengths, tokens, first, second, gains, d_qkv, d_middle, middle, hidden)

    def halve(sums):
        sums = sums.reshape(n, rows, sums.shape[1])
        got = trade(cut(sums, core ^ 1, 2), 1)
        return (cut(sums, core, 2).astype(f32) + got.astype(f32)).astype(bf16)

    kept = jnp.concatenate([halve(first_sums), halve(second_sums)], axis=2)
    for k, (place, _, partners) in enumerate(rounds[::-1]):
        ways = len(partners) + 1
        got = [trade(cut(kept, place ^ other, ways), mask) for mask, other in partners]
        kept = cut(kept, place, ways)
        if k == len(rounds) - 1:
            break
        total = kept.astype(f32)
        for piece in got:
            total = total + piece.astype(f32)
        kept = total.astype(bf16)
        if k == 0:
            kept, out, grad = lax.optimization_barrier((kept, out, grad))
    g_qkv, g_attn, g_in, g_mlp, g_first, g_second = call(
        end_kernel,
        [NEAR] * (5 + len(got)),
        [((rows, QKV), f32), ((rows, D), f32), ((rows, 2 * FF), f32), ((rows, FF), f32), ((1, rows), f32), ((1, rows), f32)],
    )(kept[0], *[piece[0] for piece in got], w_qkv, w_in, gain_attn, gain_mlp)
    return out, grad, g_qkv, g_attn, g_in, g_mlp.T, g_first.reshape(rows), g_second.reshape(rows)


def solution(mesh):
    rows = P("dp", None)
    return jax.shard_map(
        functools.partial(on_device, mesh.shape["dp"]),
        mesh=mesh,
        in_specs=(rows, P("dp"), rows, rows, rows, P(None, "dp"), P("dp"), P("dp"), rows),
        out_specs=(rows, rows, rows, rows, rows, P(None, "dp"), P("dp"), P("dp")),
        check_vma=False,
    )
```

```python
import functools

import jax
import jax.numpy as jnp
import numpy as np
from jax import lax
from jax.experimental import pallas as pl
from jax.experimental.pallas import tpu as pltpu
from jax.sharding import PartitionSpec as P

D = 256
FF = 384
HEADS = 4
HEAD_DIM = 64
BLOCK = 128
HALF = D // 2
WIDE = HEADS * BLOCK
QKV = 3 * D
LANES = 128
FIRST = QKV + D + LANES
SECOND = 2 * FF + FF
SUMS = QKV + D

rope_base = 160000.0
eps_norm = 1e-05
bf16 = jnp.bfloat16
f32 = jnp.float32


def tables():
    half_dim = HEAD_DIM // 2
    frequency = rope_base ** (-(np.arange(half_dim) * 2.0) / HEAD_DIM)
    angles = np.arange(BLOCK)[:, None] * frequency[None, :]
    angles = np.tile(angles, (1, HEADS))
    return np.cos(angles).astype(np.float32), np.sin(angles).astype(np.float32)


def mm(left, right):
    return lax.dot_general(left, right, (((1,), (0,)), ((), ())), preferred_element_type=f32)


def mm_nt(left, right):
    return lax.dot_general(left, right, (((1,), (1,)), ((), ())), preferred_element_type=f32)


def mm_tn(left, right):
    return lax.dot_general(left, right, (((0,), (0,)), ((), ())), preferred_element_type=f32)


def spread_columns(forward):
    old = lax.broadcasted_iota(jnp.int32, (D, D), 0 if forward else 1)
    new = lax.broadcasted_iota(jnp.int32, (D, D), 1 if forward else 0)
    target = ((old // 32) % 2) * HALF + (old // HEAD_DIM) * 32 + old % 32
    return jnp.where(target == new, 1.0, 0.0).astype(bf16)


def to_column(row):
    size = row.shape[1]
    here = lax.broadcasted_iota(jnp.int32, (size, size), 0)
    there = lax.broadcasted_iota(jnp.int32, (size, size), 1)
    return jnp.sum(jnp.where(here == there, row, 0.0), axis=1, keepdims=True)


def to_row(column):
    size = column.shape[0]
    here = lax.broadcasted_iota(jnp.int32, (size, size), 0)
    there = lax.broadcasted_iota(jnp.int32, (size, size), 1)
    return jnp.sum(jnp.where(here == there, column, 0.0), axis=0, keepdims=True)


def pack_kernel(w_qkv, w_attn, w_in, w_mlp, gain_attn, gain_mlp, out):
    spread = spread_columns(True)
    out[:, :D] = mm(w_qkv[:, :D], spread).astype(bf16)
    out[:, D : 2 * D] = mm(w_qkv[:, D : 2 * D], spread).astype(bf16)
    out[:, 2 * D : QKV] = w_qkv[:, 2 * D :]
    out[:, QKV : QKV + D] = w_attn[...]
    lane = lax.broadcasted_iota(jnp.int32, (out.shape[0], LANES), 1)
    gains = jnp.where(lane == 0, to_column(gain_attn[...].astype(f32)), 0.0)
    gains = jnp.where(lane == 1, to_column(gain_mlp[...].astype(f32)), gains)
    out[:, QKV + D : FIRST] = gains.astype(bf16)
    out[:, FIRST : FIRST + 2 * FF] = w_in[...]
    out[:, FIRST + 2 * FF :] = w_mlp[...]


def end_kernel(*refs):
    w_qkv, w_in, gain_attn, gain_mlp, g_qkv, g_attn, g_in, g_mlp, g_first, g_second = refs[-10:]
    total = refs[0][...].astype(f32)
    for got in refs[1:-10]:
        total = total + got[...].astype(f32)
    part = total[:, :QKV]
    g_qkv[...] = part
    g_first[...] = to_row(jnp.sum(part * w_qkv[...].astype(f32), axis=1, keepdims=True)) / gain_attn[...].astype(f32)
    g_attn[...] = total[:, QKV : QKV + D]
    part = total[:, QKV + D : QKV + D + 2 * FF]
    g_in[...] = part
    g_second[...] = to_row(jnp.sum(part * w_in[...].astype(f32), axis=1, keepdims=True)) / gain_mlp[...].astype(f32)
    g_mlp[...] = total[:, QKV + D + 2 * FF :]


def standardize(values):
    centre = values - jnp.mean(values, axis=-1, keepdims=True)
    inverse = lax.rsqrt(jnp.mean(centre * centre, axis=-1, keepdims=True) + eps_norm)
    return centre * inverse, inverse


def norm_back(d_hat, hat_rows, inverse):
    mean_one = jnp.mean(d_hat, axis=-1, keepdims=True)
    mean_two = jnp.mean(d_hat * hat_rows, axis=-1, keepdims=True)
    return inverse * (d_hat - mean_one - hat_rows * mean_two)


def stack_heads(rows, masks):
    return jnp.concatenate([rows * mask for mask in masks], axis=0)


def turn_heads(values):
    return jnp.concatenate(
        [values[:, h * BLOCK : (h + 1) * BLOCK].T for h in range(HEADS)], axis=1
    )


def head_masks():
    lane = lax.broadcasted_iota(jnp.int32, (1, D), 1)
    spread = [jnp.where((lane % HALF) // 32 == h, 1.0, 0.0).astype(bf16) for h in range(HEADS)]
    plain = [jnp.where(lane // HEAD_DIM == h, 1.0, 0.0).astype(bf16) for h in range(HEADS)]
    return spread, plain


def live_rows(lengths, count):
    row = lax.broadcasted_iota(jnp.int32, (BLOCK, 1), 0)
    live = [jnp.where(row < lengths[b], 1.0, 0.0) for b in range(count // BLOCK)]
    return jnp.concatenate(live, axis=0) > 0.5


def early_kernel(lengths, tokens, cot, hat, out_low):
    hat[...] = standardize(tokens[...].astype(f32))[0]
    live = live_rows(lengths, tokens.shape[0])
    out_low[...] = jnp.where(live, cot[...].astype(f32), 0.0).astype(bf16)


def attend_kernel(
    lengths, hat, packed, cos, sin, gains, normed, heads, shares, mixture
):
    w_qkv = packed[:, :QKV]
    here = lax.broadcasted_iota(jnp.int32, (D, D), 0) == lax.broadcasted_iota(jnp.int32, (D, D), 1)
    for k in range(2):
        column = packed[:, QKV + D + k : QKV + D + k + 1].astype(f32)
        gains[k : k + 1, :] = jnp.sum(jnp.where(here, column, 0.0), axis=0, keepdims=True)
    gain = gains[0:1, :]
    c, s = cos[...], sin[...]
    spread_masks, plain_masks = head_masks()
    key_lane = lax.broadcasted_iota(jnp.int32, (1, BLOCK), 1)
    count = hat.shape[0] // BLOCK
    for part in [slice(b * BLOCK, (b + 1) * BLOCK) for b in range(count)]:
        normed[part] = (hat[part] * gain).astype(bf16)

    def rope(base):
        both = mm(normed[...], w_qkv[:, base : base + D])
        low, high = both[:, :HALF].reshape(count, BLOCK, HALF), both[:, HALF:].reshape(count, BLOCK, HALF)
        both = jnp.concatenate([low * c - high * s, high * c + low * s], axis=2)
        return both.reshape(count * BLOCK, D)

    heads[:, :D] = (rope(0) * HEAD_DIM ** (-0.5)).astype(bf16)
    heads[:, D : 2 * D] = rope(D).astype(bf16)
    heads[:, 2 * D :] = mm(normed[...], w_qkv[:, 2 * D :]).astype(bf16)
    parts = [slice(b * BLOCK, (b + 1) * BLOCK) for b in range(count)]
    for block in parts:
        shares[block] = mm_nt(heads[block, :D], stack_heads(heads[block, D : 2 * D], spread_masks))
    for b, block in enumerate(parts):
        live = key_lane < lengths[b]
        for h in range(HEADS):
            cut = slice(h * BLOCK, (h + 1) * BLOCK)
            one = jnp.where(live, shares[block, cut], -1e30)
            grown = jnp.exp(one - jnp.max(one, axis=1, keepdims=True))
            shares[block, cut] = grown * (1.0 / jnp.sum(grown, axis=1, keepdims=True))
    for block in parts:
        mixed = mm(shares[block].astype(bf16), stack_heads(heads[block, 2 * D :], plain_masks))
        mixture[block] = mixed.astype(bf16)


def middle_kernel(
    tokens, out_low, first, second, gains, mixture, heads, shares, normed, cos, sin,
    middle, hidden, d_middle, sums, d_qkv, d_mixture, hat_two_low, d_att, d_merged,
):
    feed(
        tokens, out_low, first, second, gains, mixture,
        middle, hidden, d_middle, d_mixture, hat_two_low, d_att, d_merged,
    )
    sums[:, SUMS : SUMS + 2 * FF] = mm_tn(hat_two_low[...], d_merged[...]).astype(bf16)
    sums[:, SUMS + 2 * FF :] = mm_tn(out_low[...], hidden[...]).astype(bf16)
    attend_back(heads, shares, d_mixture, normed, mixture, d_att, cos, sin, sums, d_qkv)


def feed(
    tokens, out_low, first, second, gains, mixture,
    middle, hidden, d_middle, d_mixture, hat_two_low, d_att, d_merged,
):
    w_attn = first[:, QKV : QKV + D]
    w_in = second[:, : 2 * FF]
    w_mlp = second[:, 2 * FF :]
    gain = gains[1:2, :]
    mid = tokens[...].astype(f32) + mm(mixture[...], w_attn)
    middle[...] = mid
    hat_two, inv_two = standardize(mid)
    hat_two_low[...] = (hat_two * gain).astype(bf16)
    merged = mm(hat_two_low[...], w_in)
    inner = merged[:, :FF]
    gate = merged[:, FF:]
    cdf = 0.5 * (1.0 + lax.erf(inner * 0.7071067811865476))
    curved = inner * cdf
    slope = cdf + inner * jnp.exp(-0.5 * inner * inner) * 0.3989422804014327
    hidden[...] = (curved * gate).astype(bf16)
    out_grad = out_low[...].astype(f32)
    d_hidden = mm(out_low[...], w_mlp)
    d_merged[:, :FF] = (d_hidden * gate * slope).astype(bf16)
    d_merged[:, FF:] = (d_hidden * curved).astype(bf16)
    d_normed = mm_nt(d_merged[...], w_in)
    d_mid = out_grad + norm_back(d_normed * gain, hat_two, inv_two)
    d_middle[...] = d_mid
    d_att[...] = d_mid.astype(bf16)
    d_mixture[...] = mm_nt(d_att[...], w_attn).astype(bf16)


def attend_back(heads, shares, d_mixture, normed, mixture, d_att, cos, sin, sums, d_qkv):
    c, s = cos[...], sin[...]
    spread_masks, plain_masks = head_masks()

    def rope_back(grads):
        low, high = grads[:, :HALF], grads[:, HALF:]
        return jnp.concatenate([low * c + high * s, high * c - low * s], axis=1).astype(bf16)

    parts = [slice(b * BLOCK, (b + 1) * BLOCK) for b in range(heads.shape[0] // BLOCK)]
    d_shares = [mm_nt(d_mixture[block], stack_heads(heads[block, 2 * D :], plain_masks)) for block in parts]
    d_values = [mm(turn_heads(shares[block].astype(bf16)), stack_heads(d_mixture[block], plain_masks)) for block in parts]
    for block, d_value in zip(parts, d_values):
        d_qkv[block, 2 * D :] = d_value.astype(bf16)
    d_scores = []
    for block, d_share in zip(parts, d_shares):
        pieces = []
        for h in range(HEADS):
            cut = slice(h * BLOCK, (h + 1) * BLOCK)
            one, d_one = shares[block, cut], d_share[:, cut]
            d_one = one * (d_one - jnp.sum(one * d_one, axis=1, keepdims=True))
            pieces.append(d_one.astype(bf16))
        d_scores.append(jnp.concatenate(pieces, axis=1))
    for block, d_score in zip(parts, d_scores):
        d_qkv[block, :D] = rope_back(mm(d_score, stack_heads(heads[block, D : 2 * D], spread_masks)) * HEAD_DIM ** (-0.5))
    for block, d_score in zip(parts, d_scores):
        d_qkv[block, D : 2 * D] = rope_back(mm(turn_heads(d_score), stack_heads(heads[block, :D], spread_masks)))
    total = mm_tn(normed[...], d_qkv[...]).astype(bf16)
    spread = spread_columns(False)
    sums[:, :D] = mm(total[:, :D], spread).astype(bf16)
    sums[:, D : 2 * D] = mm(total[:, D : 2 * D], spread).astype(bf16)
    sums[:, 2 * D : QKV] = total[:, 2 * D :]
    sums[:, QKV:SUMS] = mm_tn(mixture[...], d_att[...]).astype(bf16)


def layer_kernel(
    lengths, hat, tokens, out_low, first, second, cos, sin,
    gains, middle, hidden, d_middle, sums, d_qkv,
    normed, heads, shares, mixture, d_mixture, hat_two_low, d_att, d_merged,
):
    attend_kernel(lengths, hat, first, cos, sin, gains, normed, heads, shares, mixture)
    middle_kernel(
        tokens, out_low, first, second, gains, mixture, heads, shares, normed, cos, sin,
        middle, hidden, d_middle, sums, d_qkv, d_mixture, hat_two_low, d_att, d_merged,
    )


def outputs_kernel(lengths, tokens, first, second, gains, d_qkv, d_middle, middle, hidden, out, grad):
    gain = gains[0:1, :]
    result = middle[...] + mm_nt(hidden[...], second[:, 2 * FF :])
    out[...] = jnp.where(live_rows(lengths, tokens.shape[0]), result, 0.0).astype(bf16)
    hat_one, inv_one = standardize(tokens[...].astype(f32))
    d_normed = mm_nt(d_qkv[...], first[:, :QKV])
    grad[...] = d_middle[...] + norm_back(d_normed * gain, hat_one, inv_one)


GATHER_LEAD, GATHER_LAST = (2, 3, 1), (1, 2, 3)
REDUCE_LEAD, REDUCE_LAST = (1, 2, 3), (3, 1, 2)
SMALL = pl.BlockSpec(memory_space=pltpu.SMEM)
NEAR = pl.BlockSpec(memory_space=pltpu.VMEM)


def call(kernel, in_specs, shapes, scratch=()):
    return pl.pallas_call(
        kernel,
        in_specs=in_specs,
        out_specs=[NEAR] * len(shapes),
        out_shape=[jax.ShapeDtypeStruct(shape, kind) for shape, kind in shapes],
        scratch_shapes=[pltpu.VMEM(shape, kind) for shape, kind in scratch],
        compiler_params=pltpu.CompilerParams(vmem_limit_bytes=32 * 1024 * 1024),
    )


def put(room, piece, place, column=0):
    return lax.dynamic_update_slice(room, piece[:, None], (0, place, 0, column))


def cut(room, place, ways):
    room = room.reshape(-1, ways, *room.shape[1:])
    return lax.dynamic_index_in_dim(room, place, 1, keepdims=False)


def on_device(n, tokens, lengths, w_qkv, w_attn, w_in, w_mlp, gain_attn, gain_mlp, cotangent):
    rows = D // n
    count = tokens.shape[0]
    hops = []
    while 2 ** len(hops) < n:
        hops.append(n >> (len(hops) + 1))
    hops = tuple(hops)
    lead = hops[:-1]
    me = lax.axis_index("dp")
    core = me & 1
    rounds = []
    if len(lead) % 2:
        rounds.append((me // lead[0], ((lead[0], 1),), ((lead[0], 1),)))
    for k in range(len(lead) % 2, len(lead), 2):
        one, two = lead[k], lead[k + 1]
        masks = {1: two, 2: one, 3: one ^ two}
        orders = (GATHER_LAST, REDUCE_LAST) if k + 2 == len(lead) else (GATHER_LEAD, REDUCE_LEAD)
        rounds.append(((me // two) & 3, *[tuple((masks[p], p) for p in order) for order in orders]))
    gain_attn = gain_attn.reshape(1, rows)
    gain_mlp = gain_mlp.reshape(1, rows)

    def trade(values, mask):
        return lax.ppermute(values, "dp", [(i, i ^ mask) for i in range(n)])

    held = pl.pallas_call(
        pack_kernel, out_specs=NEAR, out_shape=jax.ShapeDtypeStruct((rows, FIRST + SECOND), bf16)
    )(w_qkv, w_attn, w_in, w_mlp.T, gain_attn, gain_mlp)
    room = held[None]
    for place, partners, _ in rounds:
        got = [(trade(room, mask), other) for mask, other in partners]
        wide = put(jnp.zeros((room.shape[0], len(got) + 1, rows, FIRST + SECOND), bf16), room, place)
        for piece, other in got:
            wide = put(wide, piece, place ^ other)
        room = wide.reshape(-1, rows, FIRST + SECOND)
        if place is rounds[0][0]:
            early = lax.optimization_barrier((room, tokens, cotangent))
            room = early[0]
            hat, out_low = call(
                early_kernel, [SMALL] + [NEAR] * 2, [((count, D), f32), ((count, D), bf16)]
            )(lengths, *early[1:])
    room, hat, out_low = lax.optimization_barrier((room, hat, out_low))

    def both(half, got):
        wide = put(jnp.zeros((n // 2, 2) + half.shape[1:], bf16), half, core)
        return put(wide, got, core ^ 1).reshape(D, half.shape[2])

    first, second = room[:, :, :FIRST], room[:, :, FIRST:]
    got = trade(first, 1)
    first, second = both(first, got), both(second, trade(second, 1))

    cos, sin = tables()
    cos, sin = jnp.asarray(cos), jnp.asarray(sin)
    gains, middle, hidden, d_middle, sums, d_qkv = call(
        layer_kernel,
        [SMALL] + [NEAR] * 7,
        [((2, D), f32), ((count, D), f32), ((count, FF), bf16), ((count, D), f32), ((D, SUMS + 3 * FF), bf16), ((count, QKV), bf16)],
        [((count, D), bf16), ((count, QKV), bf16), ((count, WIDE), f32), ((count, D), bf16), ((count, D), bf16), ((count, D), bf16), ((count, D), bf16), ((count, 2 * FF), bf16)],
    )(lengths, hat, tokens, out_low, first, second, cos, sin)
    out, grad = call(
        outputs_kernel, [SMALL] + [NEAR] * 8, [((count, D), bf16), ((count, D), f32)]
    )(lengths, tokens, first, second, gains, d_qkv, d_middle, middle, hidden)

    def halve(sums):
        sums = sums.reshape(n, rows, sums.shape[1])
        got = trade(cut(sums, core ^ 1, 2), 1)
        return (cut(sums, core, 2).astype(f32) + got.astype(f32)).astype(bf16)

    kept = halve(sums)
    for k, (place, _, partners) in enumerate(rounds[::-1]):
        ways = len(partners) + 1
        got = [trade(cut(kept, place ^ other, ways), mask) for mask, other in partners]
        kept = cut(kept, place, ways)
        if k == len(rounds) - 1:
            break
        total = kept.astype(f32)
        for piece in got:
            total = total + piece.astype(f32)
        kept = total.astype(bf16)
        if k == 0:
            kept, out, grad = lax.optimization_barrier((kept, out, grad))
    g_qkv, g_attn, g_in, g_mlp, g_first, g_second = call(
        end_kernel,
        [NEAR] * (5 + len(got)),
        [((rows, QKV), f32), ((rows, D), f32), ((rows, 2 * FF), f32), ((rows, FF), f32), ((1, rows), f32), ((1, rows), f32)],
    )(kept[0], *[piece[0] for piece in got], w_qkv, w_in, gain_attn, gain_mlp)
    return out, grad, g_qkv, g_attn, g_in, g_mlp.T, g_first.reshape(rows), g_second.reshape(rows)


def solution(mesh):
    rows = P("dp", None)
    return jax.shard_map(
        functools.partial(on_device, mesh.shape["dp"]),
        mesh=mesh,
        in_specs=(rows, P("dp"), rows, rows, rows, P(None, "dp"), P("dp"), P("dp"), rows),
        out_specs=(rows, rows, rows, rows, rows, P(None, "dp"), P("dp"), P("dp")),
        check_vma=False,
    )
```
